256 devices in a mesh: cell: 8 (over x, core), tm: 32 (over y, z).
Axes of the slice: x: 4, y: 4, z: 8, core: 2. Of those that a mesh axis runs over, the one named last changes fastest.
Arguments:
- state: bfloat16 [8192, 131072], P('tm', 'cell'), may hold values from -120 to 120, as said below
- range_test: bfloat16 [8192, 128], P('tm'), may hold values from -0.0625 to 0.0625
- corange_test: bfloat16 [256, 131072], P(None, 'cell'), may hold values from -0.015625 to 0.015625
Outputs:
- basis: float32 [131072, 128], P(('cell', 'tm'))
- corange: float32 [256, 8192], P(None, 'tm')
The draws below stay inside these ranges and needn't reach their ends.
Inputs may be any that keep to these rules, and one draw needn't show every extreme that they name: state varies from cell to cell in scale.
All inputs are finite; a program needn't handle non-finite values.
Results may differ from the reference program's by a relative error of at most 0.015.
Values may be sent and summed in bfloat16 or wider, within the bound.
A program may use at most 128 MiB of HBM per device.

```python
import jax
import jax.numpy as jnp
from jax import lax

RANK = 128
CORANK = 256
STEPS = 8192
CELLS = 131072


def draw_state(key, part):
    key = jax.random.fold_in(key, 11)
    key_a, key_b = jax.random.split(key, 2)
    position = jnp.arange(CELLS, dtype=jnp.float32) / CELLS
    trend = 1.0 + 2.0 * position
    scales = jnp.exp(jax.random.uniform(key_b, (1, CELLS), jnp.float32, 0.0, jnp.log(10.0)))
    values = jnp.clip(jax.random.normal(key_a, (STEPS, CELLS), jnp.float32), -4.0, 4.0)
    return (values * scales * trend[None, :]).astype(jnp.bfloat16)


def steps_of(own_key, shape, cuts, smallest, high):
    factor_of, own = 1.0, jax.random.fold_in(own_key, 6)
    for axis_at, shards_of in cuts:
        steps = jnp.exp(jax.random.uniform(jax.random.fold_in(own, axis_at), (shards_of,), jnp.float32, smallest / len(cuts), high / len(cuts)))
        factor_of = factor_of * jnp.repeat(steps, shape[axis_at] // shards_of).reshape([-1 if axis == axis_at else 1 for axis in range(len(shape))])
    return factor_of


def noise(own_key, extent, scale, most, pieces=(), kind=jnp.bfloat16):
    loudness = steps_of(own_key, extent, pieces, -0.22, 0.18) if pieces else 1.0
    entries = jax.random.normal(own_key, extent, jnp.float32) * scale * loudness
    return jnp.minimum(jnp.maximum(entries, -most), most).astype(kind)


def setup_inputs(seed: int = 0) -> dict:
    keys = jax.random.split(jax.random.key(seed), 4)
    state = draw_state(jax.random.fold_in(keys[3], 71), 0)
    range_test = noise(keys[1], (STEPS, RANK), STEPS ** -0.5, 0.0625, ((0, 32),))
    corange_test = noise(keys[2], (CORANK, CELLS), CELLS ** -0.5, 0.015625, ((1, 8),))
    return dict(state=state, range_test=range_test, corange_test=corange_test)


def reference(state, range_test, corange_test):
    sketch = lax.dot_general(state.astype(jnp.float32), range_test.astype(jnp.float32), (((0,), (0,)), ((), ())), preferred_element_type=jnp.float32)
    corange = lax.dot_general(corange_test.astype(jnp.float32), state.astype(jnp.float32), (((1,), (1,)), ((), ())), preferred_element_type=jnp.float32)
    gram = jnp.dot(sketch.T, sketch, precision=lax.Precision.HIGHEST)
    lower = jnp.linalg.cholesky(gram)
    solved = lax.linalg.triangular_solve(lower, sketch, left_side=False, lower=True, transpose_a=True)
    basis = solved * jnp.sqrt(jnp.float32(CELLS))
    return (basis, corange)
```

```python
import functools

import jax
import jax.numpy as jnp
from jax import lax
from jax.experimental import pallas as pl
from jax.experimental.pallas import tpu as pltpu
from jax.sharding import PartitionSpec as P

MESH = pl.DeviceIdType.MESH
F32, BF16 = jnp.float32, jnp.bfloat16
NY, NZ, NC = 4, 8, 8
RANK, STEPS, OWN, HALF = 128, 256, 512, 256
A = 80
SCALE = 32768.0
ORDER = (4, 3, 5, 2, 6, 1, 7, 0)


def encode(x):
    s = x * x
    return (s * x * jnp.abs(x)).astype(BF16)


def decode(y):
    y = y.astype(F32)
    r = lax.rsqrt(lax.rsqrt(jnp.maximum(jnp.abs(y), 1.2e-38)))
    return jnp.where(y < 0, -r, r)


def span(h):
    return pl.ds(h * HALF, HALF)


class Ring:
    def __init__(self, lead, snd, rcv, ssem, rsem, plus, minus, targets):
        self.lead, self.snd, self.rcv = lead, snd, rcv
        self.ssem, self.rsem = ssem, rsem
        self.ids = {1: plus, -1: minus}
        self.targets = targets

    def copy(self, m):
        i = self.lead + (m,)
        return pltpu.make_async_remote_copy(
            self.snd.at[i], self.rcv.at[i], self.ssem.at[i], self.rsem.at[i],
            device_id=self.ids[self.targets[m]], device_id_type=MESH,
        )

    def put(self, m, value):
        self.snd[self.lead + (m,)] = encode(value)

    def send(self, m):
        self.copy(m).start()

    def take(self, m):
        self.copy(m).wait_recv()
        return decode(self.rcv[self.lead + (m,)])


DIR4 = (1, -1, 1, -1, 1, -1)
DIR8 = (1,) * 7 + (-1,) * 7


def gather_kernel(state_hbm, r_ref, c_hbm, st_ref, gram_ref, cor_ref,
                  rt, sbuf, cbuf, part, cor,
                  sa1, ra1, sa2, ra2, sb1, rb1, sb2, rb2, crecv, cfull, cown,
                  gpart, g1, g2, g3, g4, gown,
                  state_sem, c_sem, ssa1, rsa1, ssa2, rsa2, ssb1, rsb1, ssb2, rsb2,
                  sc, rc, sg1, rg1, sg2, rg2, sg3, rg3, sg4, rg4):
    c, t = lax.axis_index("cell"), lax.axis_index("tm")
    y, z = t // NZ, lax.rem(t, NZ)

    def at_y(o):
        return (c, lax.rem(y + o, NY) * NZ + z)

    def at_z(o):
        return (c, y * NZ + lax.rem(z + o, NZ))

    def at_c(o):
        return (lax.rem(c + o, NC), t)

    barrier = pltpu.get_barrier_semaphore()
    peers = [at_y(o) for o in range(1, NY)] + [at_z(o) for o in range(1, NZ)] + [at_c(o) for o in range(1, NC)]
    for p in peers:
        pl.semaphore_signal(barrier, inc=1, device_id=p, device_id_type=MESH)

    def load(hbm, buf, sem, zo, yo):
        chunk = lax.rem(y + yo, NY) * NZ + lax.rem(z + zo, NZ)
        cols = pl.ds(pl.multiple_of(chunk * OWN, OWN), OWN)
        return pltpu.make_async_copy(hbm.at[:, cols], buf.at[zo, yo], sem.at[zo, yo])

    for zo in ORDER:
        for yo in range(NY):
            load(state_hbm, sbuf, state_sem, zo, yo).start()
    for zo in ORDER:
        for yo in range(NY):
            load(c_hbm, cbuf, c_sem, zo, yo).start()

    rt[...] = (r_ref[...].astype(F32) * SCALE).T.astype(BF16)

    ring_a1 = [Ring((zo,), sa1, ra1, ssa1, rsa1, at_y(1), at_y(NY - 1), DIR4) for zo in range(NZ)]
    ring_a2 = Ring((), sa2, ra2, ssa2, rsa2, at_z(1), at_z(NZ - 1), DIR8)
    ring_b1 = [Ring((yo,), sb1, rb1, ssb1, rsb1, at_z(1), at_z(NZ - 1), DIR8) for yo in range(NY)]
    ring_b2 = Ring((), sb2, rb2, ssb2, rsb2, at_y(1), at_y(NY - 1), DIR4)

    def pa(zo, yo, h):
        return part[zo, yo, 0:A, span(h)]

    def pb(zo, yo, h):
        return part[zo, yo, A:RANK, span(h)]

    def multiply(zo):
        @pl.loop(0, NY)
        def _(yo):
            load(state_hbm, sbuf, state_sem, zo, yo).wait()
            part[zo, yo] = jnp.dot(rt[...], sbuf[zo, yo], preferred_element_type=F32)

    def raw4(ring, own):
        for m, (yo, h) in enumerate(((2, 0), (2, 1), (1, 1), (3, 0))):
            ring.put(m, own(yo, h))
            ring.send(m)

    def acc4(ring, own):
        for m, frm, yo, h in ((4, 0, 1, 0), (5, 1, 3, 1)):
            ring.put(m, own(yo, h) + ring.take(frm))
            ring.send(m)

    def fin4(ring, own):
        return (own(0, 0) + ring.take(3) + ring.take(4), own(0, 1) + ring.take(2) + ring.take(5))

    def far8(ring, own):
        for m, h in ((0, 0), (7, 1)):
            ring.put(m, own(4, h))
            ring.send(m)

    def raw8(ring, own, plus):
        m, zo, h = (4, 3, 1) if plus else (11, 5, 0)
        ring.put(m, own(zo, h))
        ring.send(m)

    def acc8(ring, own, d):
        todo = [(4 - d, d, 0), (11 - d, NZ - d, 1)]
        if d < 3:
            todo += [(7 - d, d, 1), (14 - d, NZ - d, 0)]
        for m, zo, h in todo:
            ring.put(m, own(zo, h) + ring.take(m - 1))
            ring.send(m)

    def fin8(ring, own):
        return (own(0, 0) + ring.take(3) + ring.take(13), own(0, 1) + ring.take(6) + ring.take(10))

    def own_a1(zo):
        return lambda yo, h: pa(zo, yo, h)

    def own_a2(zo, h):
        return pa(zo, 0, h)

    def own_b1(yo):
        return lambda zo, h: pb(zo, yo, h)

    def own_b2(yo, h):
        return pb(0, yo, h)

    def sends(g):
        zo = ORDER[g]
        raw4(ring_a1[zo], own_a1(zo))

    def group(g):
        zo = ORDER[g]
        multiply(zo)
        if zo == 4:
            pl.semaphore_wait(barrier, len(peers))
            for yo in range(NY):
                far8(ring_b1[yo], own_b1(yo))
        if zo in (3, 5):
            for yo in range(NY):
                raw8(ring_b1[yo], own_b1(yo), zo == 3)

    def acc(g):
        zo = ORDER[g]
        acc4(ring_a1[zo], own_a1(zo))

    def y_done(g):
        zo = ORDER[g]
        lo, hi = fin4(ring_a1[zo], own_a1(zo))
        part[zo, 0, 0:A, span(0)] = lo
        part[zo, 0, 0:A, span(1)] = hi
        if zo == 4:
            far8(ring_a2, own_a2)
        if zo in (3, 5):
            raw8(ring_a2, own_a2, zo == 3)

    def b_step(d, yos):
        for yo in yos:
            acc8(ring_b1[yo], own_b1(yo), d)

    def b_done(yos):
        for yo in yos:
            lo, hi = fin8(ring_b1[yo], own_b1(yo))
            part[0, yo, A:RANK, span(0)] = lo
            part[0, yo, A:RANK, span(1)] = hi

    cor[...] = jnp.zeros_like(cor)

    def correlate(gs):
        for g in gs:
            zo = ORDER[g]

            @pl.loop(0, NY)
            def _(yo):
                load(c_hbm, cbuf, c_sem, zo, yo).wait()
                cor[...] += lax.dot_general(
                    cbuf[zo, yo], sbuf[zo, yo], (((1,), (1,)), ((), ())), preferred_element_type=F32
                )

    rows = 256 // NC

    def cor_rs(o):
        at = pl.ds(pl.multiple_of(lax.rem(c + o, NC) * rows, rows), rows)
        return pltpu.make_async_remote_copy(
            cor.at[at], crecv.at[o - 1], sc.at[0, o - 1], rc.at[0, o - 1], device_id=at_c(o), device_id_type=MESH)

    def cor_ag(o):
        return pltpu.make_async_remote_copy(
            cown, cfull.at[o - 1], sc.at[1, o - 1], rc.at[1, o - 1], device_id=at_c(o), device_id_type=MESH)

    mine = pl.ds(pl.multiple_of(c * rows, rows), rows)

    group(0)
    sends(0)
    group(1)
    sends(1)
    group(2)
    sends(2)
    acc(0)
    b_step(3, (0, 1, 2, 3))
    group(3)
    sends(3)
    group(4)
    acc(1)
    y_done(0)
    b_step(2, (0, 1))
    sends(4)
    group(5)
    correlate((0, 1))
    acc(2)
    y_done(1)
    b_step(2, (2, 3))
    sends(5)
    group(6)
    correlate((2, 3))
    acc(3)
    y_done(2)
    acc8(ring_a2, own_a2, 3)
    b_step(1, (0, 1))
    sends(6)
    group(7)
    correlate((4, 5))
    acc(4)
    y_done(3)
    b_step(1, (2, 3))
    sends(7)
    correlate((6, 7))
    for o in range(1, NC):
        cor_rs(o).start()
    acc(5)
    y_done(4)
    acc8(ring_a2, own_a2, 2)
    b_done((0, 1))
    acc(6)
    y_done(5)
    b_done((2, 3))
    raw4(ring_b2, own_b2)
    total = cor[mine]
    for o in range(1, NC):
        cor_rs(o).wait_recv()
        total = total + crecv[o - 1]
    cown[...] = total
    for o in range(1, NC):
        cor_ag(o).start()
    acc(7)
    y_done(6)
    acc8(ring_a2, own_a2, 1)
    acc4(ring_b2, own_b2)
    y_done(7)
    blo, bhi = fin4(ring_b2, own_b2)
    alo, ahi = fin8(ring_a2, own_a2)
    st_ref[A:RANK, span(0)] = blo
    st_ref[A:RANK, span(1)] = bhi
    st_ref[0:A, span(0)] = alo
    st_ref[0:A, span(1)] = ahi

    sk = st_ref[...]
    gpart[...] = lax.dot_general(sk, sk, (((1,), (1,)), ((), ())),
                                 precision=lax.Precision.HIGHEST, preferred_element_type=F32)
    gr = RANK // NC
    mine_g = pl.ds(pl.multiple_of(c * gr, gr), gr)

    def rs1(o):
        at = pl.ds(pl.multiple_of(lax.rem(c + o, NC) * gr, gr), gr)
        return pltpu.make_async_remote_copy(
            gpart.at[at], g1.at[o - 1], sg1.at[o - 1], rg1.at[o - 1], device_id=at_c(o), device_id_type=MESH)

    def ag2(o):
        return pltpu.make_async_remote_copy(
            gown.at[0], g2.at[o - 1], sg2.at[o - 1], rg2.at[o - 1], device_id=at_y(o), device_id_type=MESH)

    def ag3(o):
        return pltpu.make_async_remote_copy(
            gown.at[1], g3.at[o - 1], sg3.at[o - 1], rg3.at[o - 1], device_id=at_z(o), device_id_type=MESH)

    def ag4(o):
        return pltpu.make_async_remote_copy(
            gown.at[2], g4.at[o - 1], sg4.at[o - 1], rg4.at[o - 1], device_id=at_c(o), device_id_type=MESH)

    def phase(make, n, own, recv, slot):
        total = own
        for o in range(1, n):
            make(o).wait_recv()
            total = total + recv[o - 1]
        gown[slot] = total
        return total

    for o in range(1, NC):
        rs1(o).start()
    total = phase(rs1, NC, gpart[mine_g], g1, 0)
    for o in range(1, NY):
        ag2(o).start()
    total = phase(ag2, NY, total, g2, 1)
    for o in range(1, NZ):
        ag3(o).start()
    total = phase(ag3, NZ, total, g3, 2)
    for o in range(1, NC):
        ag4(o).start()
    gram_ref[mine_g] = total

    cor_ref[mine] = cown[...]
    for o in range(1, NC):
        cor_ag(o).wait_recv()
        at = pl.ds(pl.multiple_of(lax.rem(c + NC - o, NC) * rows, rows), rows)
        cor_ref[at] = cfull[o - 1]
    for o in range(1, NC):
        ag4(o).wait_recv()
        at = pl.ds(pl.multiple_of(lax.rem(c + NC - o, NC) * gr, gr), gr)
        gram_ref[at] = g4[o - 1]

    for ring in ring_a1 + [ring_b2]:
        for m in range(6):
            ring.copy(m).wait_send()
    for ring in ring_b1 + [ring_a2]:
        for m in range(14):
            ring.copy(m).wait_send()
    for o in range(1, NC):
        cor_rs(o).wait_send()
        cor_ag(o).wait_send()
        rs1(o).wait_send()
        ag4(o).wait_send()
    for o in range(1, NY):
        ag2(o).wait_send()
    for o in range(1, NZ):
        ag3(o).wait_send()


def gather(state, range_test, corange_test):
    dma = pltpu.SemaphoreType.DMA
    B = RANK - A

    def bf(*s):
        return pltpu.VMEM(s, BF16)

    def fl(*s):
        return pltpu.VMEM(s, F32)

    vmem = pl.BlockSpec(memory_space=pltpu.VMEM)
    hbm = pl.BlockSpec(memory_space=pl.ANY)
    return pl.pallas_call(
        gather_kernel,
        name="sketch_sums",
        out_shape=(
            jax.ShapeDtypeStruct((RANK, OWN), F32),
            jax.ShapeDtypeStruct((RANK, RANK), F32),
            jax.ShapeDtypeStruct((256, 256), F32),
        ),
        in_specs=[hbm, vmem, hbm],
        out_specs=(vmem, vmem, vmem),
        scratch_shapes=[
            bf(RANK, STEPS), bf(NZ, NY, STEPS, OWN), bf(NZ, NY, 256, OWN), fl(NZ, NY, RANK, OWN), fl(256, 256),
            bf(NZ, 6, A, HALF), bf(NZ, 6, A, HALF), bf(14, A, HALF), bf(14, A, HALF),
            bf(NY, 14, B, HALF), bf(NY, 14, B, HALF), bf(6, B, HALF), bf(6, B, HALF),
            fl(7, 32, 256), fl(7, 32, 256), fl(32, 256),
            fl(RANK, RANK), fl(7, 16, RANK), fl(3, 16, RANK), fl(7, 16, RANK), fl(7, 16, RANK), fl(3, 16, RANK),
            dma((NZ, NY)), dma((NZ, NY)),
            dma((NZ, 6)), dma((NZ, 6)), dma((14,)), dma((14,)),
            dma((NY, 14)), dma((NY, 14)), dma((6,)), dma((6,)),
            dma((2, 7)), dma((2, 7)),
            dma((7,)), dma((7,)), dma((3,)), dma((3,)), dma((7,)), dma((7,)), dma((7,)), dma((7,)),
        ],
        compiler_params=pltpu.CompilerParams(
            collective_id=1, has_side_effects=True, vmem_limit_bytes=56 << 20),
    )(state, range_test, corange_test)


def factor_kernel(scale, gram_ref, st_ref, out_ref, w_ref):
    n = RANK
    lane = lax.broadcasted_iota(jnp.int32, (1, n), 1)
    sub = lax.broadcasted_iota(jnp.int32, (n, 1), 0)
    w = gram_ref[...]
    for k in range(n - 1):
        top = (k + 1) // 8 * 8
        low = w[top:]
        row = w[k:k + 1]
        pivot = w[k:k + 1, k:k + 1]
        col = low[:, k:k + 1]
        mult = jnp.where(sub[top:] > k, col / pivot, 0.0)
        hit = (lane == k) & (sub[top:] > k)
        row = jnp.where(lane == k, 1.0, row)
        low = jnp.where(hit, 0.0, low) - mult * row
        w = jnp.concatenate([w[:top], low], axis=0) if top else low
    diag = jnp.sum(jnp.where(lane == sub, w, 0.0), axis=1, keepdims=True)
    unit = jnp.where(lane < sub, w, jnp.where(lane == sub, 1.0, 0.0))
    w_ref[...] = unit * (scale * lax.rsqrt(diag))
    out_ref[...] = lax.dot_general(st_ref[...], w_ref[...], (((0,), (1,)), ((), ())),
                                   precision=lax.Precision.HIGHEST, preferred_element_type=F32)


def factor(gram, st, scale):
    vmem = pl.BlockSpec(memory_space=pltpu.VMEM)
    return pl.pallas_call(
        functools.partial(factor_kernel, scale),
        name="factor",
        out_shape=jax.ShapeDtypeStruct((OWN, RANK), F32),
        in_specs=[vmem, vmem],
        out_specs=vmem,
        scratch_shapes=[pltpu.VMEM((RANK, RANK), F32)],
        compiler_params=pltpu.CompilerParams(vmem_limit_bytes=32 << 20),
    )(gram, st)


def on_device(state, range_test, corange_test):
    total_cells = state.shape[1] * NC
    st, gram, corange = gather(state, range_test, corange_test)
    basis = factor(gram, st, float(total_cells) ** 0.5)
    return (basis, corange)


def solution(mesh):
    return jax.shard_map(
        on_device,
        mesh=mesh,
        in_specs=(P("tm", "cell"), P("tm", None), P(None, "cell")),
        out_specs=(P(("cell", "tm"), None), P(None, "tm")),
        check_vma=False,
    )
```

```python
import functools

import jax
import jax.numpy as jnp
from jax import lax
from jax.experimental import pallas as pl
from jax.experimental.pallas import tpu as pltpu
from jax.sharding import PartitionSpec as P

MESH = pl.DeviceIdType.MESH
F32, BF16 = jnp.float32, jnp.bfloat16
NY, NZ, NC = 4, 8, 8
RANK, STEPS, OWN, HALF = 128, 256, 512, 256
A = 80
SCALE = 32768.0
ORDER = (4, 3, 5, 2, 6, 1, 7, 0)
FAR_C = (4, 5, 3, 2, 6, 7, 1)

SCHEDULE = (
    ("g", 0), ("s", 0), ("g", 1), ("g", 2), ("s", 1), ("g", 3), ("c", 2), ("b3", 1), ("c", 1), ("s", 2),
    ("a", 0), ("s", 3), ("g", 4), ("b3", 0), ("b3", 3), ("c", 4), ("g", 5), ("g", 6), ("b3", 2), ("b2", 1),
    ("g", 7), ("a", 1), ("s", 4), ("b2", 0), ("b2", 2), ("c", 6), ("b2", 3), ("a", 2), ("y", 0), ("c", 0),
    ("c", 5), ("c", 7), ("c", 3), ("cs",), ("y", 1), ("a", 3), ("b1", 2), ("b1", 0), ("s", 5), ("y", 2),
    ("A3",), ("b1", 3), ("s", 6), ("a", 4), ("b1", 1), ("y", 3), ("a", 5), ("b0", 0), ("cq",), ("a", 6),
    ("s", 7), ("b0", 2), ("b0", 3), ("y", 4), ("A2",), ("b0", 1), ("y", 5), ("r",), ("y", 6), ("a", 7),
    ("A1",), ("q",), ("y", 7),
)


def encode(x):
    s = x * x
    return (s * x * jnp.abs(x)).astype(BF16)


def decode(y):
    y = y.astype(F32)
    r = lax.rsqrt(lax.rsqrt(jnp.maximum(jnp.abs(y), 1.2e-38)))
    return jnp.where(y < 0, -r, r)


def span(h):
    return pl.ds(h * HALF, HALF)


class Ring:
    def __init__(self, lead, snd, rcv, ssem, rsem, plus, minus, targets):
        self.lead, self.snd, self.rcv = lead, snd, rcv
        self.ssem, self.rsem = ssem, rsem
        self.ids = {1: plus, -1: minus}
        self.targets = targets

    def copy(self, m):
        i = self.lead + (m,)
        return pltpu.make_async_remote_copy(
            self.snd.at[i], self.rcv.at[i], self.ssem.at[i], self.rsem.at[i],
            device_id=self.ids[self.targets[m]], device_id_type=MESH,
        )

    def put(self, m, value):
        self.snd[self.lead + (m,)] = encode(value)

    def send(self, m):
        self.copy(m).start()

    def take(self, m):
        self.copy(m).wait_recv()
        return decode(self.rcv[self.lead + (m,)])


DIR4 = (1, -1, 1, -1, 1, -1)
DIR8 = (1,) * 7 + (-1,) * 7


def gather_kernel(state_hbm, r_ref, c_hbm, st_out, gram_out, cor_out,
                  rt, sbuf, cbuf, part, cor,
                  sa1, ra1, sa2, ra2, sb1, rb1, sb2, rb2, crecv, cfull,
                  st, gpart, g1, g2, g3, g4,
                  state_sem, c_sem, ssa1, rsa1, ssa2, rsa2, ssb1, rsb1, ssb2, rsb2,
                  sc, rc, sg1, rg1, sg2, rg2, sg3, rg3, sg4, rg4, out_sem):
    c, t = lax.axis_index("cell"), lax.axis_index("tm")
    y, z = t // NZ, lax.rem(t, NZ)

    def at_y(o):
        return (c, lax.rem(y + o, NY) * NZ + z)

    def at_z(o):
        return (c, y * NZ + lax.rem(z + o, NZ))

    def at_c(o):
        return (lax.rem(c + o, NC), t)

    barrier = pltpu.get_barrier_semaphore()
    peers = [at_y(o) for o in range(1, NY)] + [at_z(o) for o in range(1, NZ)] + [at_c(o) for o in range(1, NC)]
    for p in peers:
        pl.semaphore_signal(barrier, inc=1, device_id=p, device_id_type=MESH)

    def load(hbm, buf, sem, zo, yo):
        chunk = lax.rem(y + yo, NY) * NZ + lax.rem(z + zo, NZ)
        cols = pl.ds(pl.multiple_of(chunk * OWN, OWN), OWN)
        return pltpu.make_async_copy(hbm.at[:, cols], buf.at[zo, yo], sem.at[zo, yo])

    for zo in ORDER:
        for yo in range(NY):
            load(state_hbm, sbuf, state_sem, zo, yo).start()
    for zo in ORDER:
        for yo in range(NY):
            load(c_hbm, cbuf, c_sem, zo, yo).start()

    rt[...] = (r_ref[...].astype(F32) * SCALE).T.astype(BF16)

    ring_a1 = [Ring((zo,), sa1, ra1, ssa1, rsa1, at_y(1), at_y(NY - 1), DIR4) for zo in range(NZ)]
    ring_a2 = Ring((), sa2, ra2, ssa2, rsa2, at_z(1), at_z(NZ - 1), DIR8)
    ring_b1 = [Ring((yo,), sb1, rb1, ssb1, rsb1, at_z(1), at_z(NZ - 1), DIR8) for yo in range(NY)]
    ring_b2 = Ring((), sb2, rb2, ssb2, rsb2, at_y(1), at_y(NY - 1), DIR4)

    def pa(zo, yo, h):
        return part[zo, yo, 0:A, span(h)]

    def pb(zo, yo, h):
        return part[zo, yo, A:RANK, span(h)]

    def multiply(zo):
        @pl.loop(0, NY)
        def _(yo):
            load(state_hbm, sbuf, state_sem, zo, yo).wait()
            part[zo, yo] = jnp.dot(rt[...], sbuf[zo, yo], preferred_element_type=F32)

    def raw4(ring, own):
        for m, (yo, h) in enumerate(((2, 0), (2, 1), (1, 1), (3, 0))):
            ring.put(m, own(yo, h))
            ring.send(m)

    def acc4(ring, own):
        for m, frm, yo, h in ((4, 0, 1, 0), (5, 1, 3, 1)):
            ring.put(m, own(yo, h) + ring.take(frm))
            ring.send(m)

    def fin4(ring, own):
        return (own(0, 0) + ring.take(3) + ring.take(4), own(0, 1) + ring.take(2) + ring.take(5))

    def far8(ring, own):
        for m, h in ((0, 0), (7, 1)):
            ring.put(m, own(4, h))
            ring.send(m)

    def raw8(ring, own, plus):
        m, zo, h = (4, 3, 1) if plus else (11, 5, 0)
        ring.put(m, own(zo, h))
        ring.send(m)

    def acc8(ring, own, d):
        todo = [(4 - d, d, 0), (11 - d, NZ - d, 1)]
        if d < 3:
            todo += [(7 - d, d, 1), (14 - d, NZ - d, 0)]
        for m, zo, h in todo:
            ring.put(m, own(zo, h) + ring.take(m - 1))
            ring.send(m)

    def fin8(ring, own):
        return (own(0, 0) + ring.take(3) + ring.take(13), own(0, 1) + ring.take(6) + ring.take(10))

    def own_a1(zo):
        return lambda yo, h: pa(zo, yo, h)

    def own_a2(zo, h):
        return pa(zo, 0, h)

    def own_b1(yo):
        return lambda zo, h: pb(zo, yo, h)

    def own_b2(yo, h):
        return pb(0, yo, h)

    def sends(g):
        zo = ORDER[g]
        raw4(ring_a1[zo], own_a1(zo))

    def group(g):
        zo = ORDER[g]
        multiply(zo)
        if zo == 4:
            pl.semaphore_wait(barrier, len(peers))
            for yo in range(NY):
                far8(ring_b1[yo], own_b1(yo))
        if zo in (3, 5):
            for yo in range(NY):
                raw8(ring_b1[yo], own_b1(yo), zo == 3)

    def acc(g):
        zo = ORDER[g]
        acc4(ring_a1[zo], own_a1(zo))

    def y_done(g):
        zo = ORDER[g]
        lo, hi = fin4(ring_a1[zo], own_a1(zo))
        part[zo, 0, 0:A, span(0)] = lo
        part[zo, 0, 0:A, span(1)] = hi
        if zo == 4:
            far8(ring_a2, own_a2)
        if zo in (3, 5):
            raw8(ring_a2, own_a2, zo == 3)

    def b_step(d):
        return lambda yo: acc8(ring_b1[yo], own_b1(yo), d)

    def b_done(yo):
        lo, hi = fin8(ring_b1[yo], own_b1(yo))
        part[0, yo, A:RANK, span(0)] = lo
        part[0, yo, A:RANK, span(1)] = hi

    cor[...] = jnp.zeros_like(cor)

    def correlate(g):
        zo = ORDER[g]

        @pl.loop(0, NY)
        def _(yo):
            load(c_hbm, cbuf, c_sem, zo, yo).wait()
            cor[...] += lax.dot_general(
                cbuf[zo, yo], sbuf[zo, yo], (((1,), (1,)), ((), ())), preferred_element_type=F32
            )

    rows = 256 // NC

    def strip(i, n):
        return pl.ds(pl.multiple_of(i * n, n), n)

    def near_c(o):
        return lax.rem(c + o, NC)

    def cor_rs(o):
        return pltpu.make_async_remote_copy(
            cor.at[strip(near_c(o), rows)], crecv.at[o - 1], sc.at[0, o - 1], rc.at[0, o - 1],
            device_id=at_c(o), device_id_type=MESH)

    def cor_ag(o, owner):
        return pltpu.make_async_remote_copy(
            cfull.at[strip(owner, rows)], cfull.at[strip(owner, rows)], sc.at[1, o - 1], rc.at[1, owner],
            device_id=at_c(o), device_id_type=MESH)

    def cor_send():
        for o in FAR_C:
            cor_rs(o).start()

    def cor_sum():
        total = cor[strip(c, rows)]
        for o in range(1, NC):
            cor_rs(o).wait_recv()
            total = total + crecv[o - 1]
        cfull[strip(c, rows)] = total
        for o in FAR_C:
            cor_ag(o, c).start()

    acts = {
        "g": group, "s": sends, "a": acc, "y": y_done, "c": correlate, "cs": cor_send, "cq": cor_sum,
        "b3": b_step(3), "b2": b_step(2), "b1": b_step(1), "b0": b_done,
        "A3": lambda: acc8(ring_a2, own_a2, 3),
        "A2": lambda: acc8(ring_a2, own_a2, 2),
        "A1": lambda: acc8(ring_a2, own_a2, 1),
        "r": lambda: raw4(ring_b2, own_b2),
        "q": lambda: acc4(ring_b2, own_b2),
    }
    for act, *which in SCHEDULE:
        acts[act](*which)

    blo, bhi = fin4(ring_b2, own_b2)
    st[A:RANK, span(0)] = blo
    st[A:RANK, span(1)] = bhi
    alo, ahi = fin8(ring_a2, own_a2)
    st[0:A, span(0)] = alo
    st[0:A, span(1)] = ahi

    sk = st[...]
    gpart[...] = lax.dot_general(sk, sk, (((1,), (1,)), ((), ())),
                                 precision=lax.Precision.HIGHEST, preferred_element_type=F32)
    gr = RANK // NC

    def rs1(o):
        return pltpu.make_async_remote_copy(
            gpart.at[strip(near_c(o), gr)], g1.at[o - 1], sg1.at[o - 1], rg1.at[o - 1],
            device_id=at_c(o), device_id_type=MESH)

    def ag2(o, owner):
        return pltpu.make_async_remote_copy(
            g2.at[owner], g2.at[owner], sg2.at[o - 1], rg2.at[owner], device_id=at_y(o), device_id_type=MESH)

    def ag3(o, owner):
        return pltpu.make_async_remote_copy(
            g3.at[owner], g3.at[owner], sg3.at[o - 1], rg3.at[owner], device_id=at_z(o), device_id_type=MESH)

    def ag4(o, owner):
        return pltpu.make_async_remote_copy(
            g4.at[strip(owner, gr)], g4.at[strip(owner, gr)], sg4.at[o - 1], rg4.at[owner],
            device_id=at_c(o), device_id_type=MESH)

    for o in FAR_C:
        rs1(o).start()
    outs = [pltpu.make_async_copy(st, st_out, out_sem.at[0]),
            pltpu.make_async_copy(cfull, cor_out, out_sem.at[1]),
            pltpu.make_async_copy(g4, gram_out, out_sem.at[2])]
    outs[0].start()
    total = gpart[strip(c, gr)]
    for o in FAR_C[::-1]:
        rs1(o).wait_recv()
        total = total + g1[o - 1]
    g2[y] = total
    for o in (2, 1, 3):
        ag2(o, y).start()
    for o in range(1, NC):
        cor_ag(o, near_c(o)).wait_recv()
    outs[1].start()
    for o in (1, 3, 2):
        ag2(o, lax.rem(y + o, NY)).wait_recv()
    total = g2[0]
    for i in range(1, NY):
        total = total + g2[i]
    g3[z] = total
    for o in (4, 3, 5, 2, 6, 1, 7):
        ag3(o, z).start()
    for ring in ring_a1 + [ring_b2]:
        for m in range(6):
            ring.copy(m).wait_send()
    for ring in ring_b1 + [ring_a2]:
        for m in range(14):
            ring.copy(m).wait_send()
    for o in range(1, NC):
        cor_rs(o).wait_send()
        cor_ag(o, c).wait_send()
        rs1(o).wait_send()
    for o in range(1, NY):
        ag2(o, y).wait_send()
    for o in (1, 7, 2, 6, 3, 5, 4):
        ag3(o, lax.rem(z + o, NZ)).wait_recv()
    total = g3[0]
    for i in range(1, NZ):
        total = total + g3[i]
    g4[strip(c, gr)] = total
    for o in FAR_C:
        ag4(o, c).start()
    for o in range(1, NZ):
        ag3(o, z).wait_send()
    outs[0].wait()
    outs[1].wait()
    for o in FAR_C[::-1]:
        ag4(o, near_c(o)).wait_recv()
    outs[2].start()
    for o in range(1, NC):
        ag4(o, c).wait_send()
    outs[2].wait()


def gather(state, range_test, corange_test):
    dma = pltpu.SemaphoreType.DMA
    B = RANK - A

    def bf(*s):
        return pltpu.VMEM(s, BF16)

    def fl(*s):
        return pltpu.VMEM(s, F32)

    vmem = pl.BlockSpec(memory_space=pltpu.VMEM)
    hbm = pl.BlockSpec(memory_space=pl.ANY)
    return pl.pallas_call(
        gather_kernel,
        name="sketch_sums",
        out_shape=(
            jax.ShapeDtypeStruct((RANK, OWN), F32),
            jax.ShapeDtypeStruct((RANK, RANK), F32),
            jax.ShapeDtypeStruct((256, 256), F32),
        ),
        in_specs=[hbm, vmem, hbm],
        out_specs=(hbm, hbm, hbm),
        scratch_shapes=[
            bf(RANK, STEPS), bf(NZ, NY, STEPS, OWN), bf(NZ, NY, 256, OWN), fl(NZ, NY, RANK, OWN), fl(256, 256),
            bf(NZ, 6, A, HALF), bf(NZ, 6, A, HALF), bf(14, A, HALF), bf(14, A, HALF),
            bf(NY, 14, B, HALF), bf(NY, 14, B, HALF), bf(6, B, HALF), bf(6, B, HALF),
            fl(7, 32, 256), fl(256, 256),
            fl(RANK, OWN), fl(RANK, RANK), fl(7, 16, RANK), fl(NY, 16, RANK), fl(NZ, 16, RANK), fl(RANK, RANK),
            dma((NZ, NY)), dma((NZ, NY)),
            dma((NZ, 6)), dma((NZ, 6)), dma((14,)), dma((14,)),
            dma((NY, 14)), dma((NY, 14)), dma((6,)), dma((6,)),
            dma((2, 7)), dma((2, NC)),
            dma((7,)), dma((7,)), dma((3,)), dma((NY,)), dma((7,)), dma((NZ,)), dma((7,)), dma((NC,)), dma((3,)),
        ],
        compiler_params=pltpu.CompilerParams(
            collective_id=1, has_side_effects=True, vmem_limit_bytes=56 << 20),
    )(state, range_test, corange_test)


def inverse_factor(w, scale):
    lane = lax.broadcasted_iota(jnp.int32, (8, RANK), 1)
    sub = lax.broadcasted_iota(jnp.int32, (8, RANK), 0)
    full = (8, RANK)
    out = []
    for b in range(RANK // 8):
        k = 8 * b
        inside = (lane >= k) & (lane < k + 8)
        cols = [jnp.broadcast_to(w[b][:, k + j:k + j + 1], full) for j in range(8)]
        p = [[jnp.broadcast_to(cols[j][i:i + 1], full) for j in range(i + 1)] for i in range(8)]
        l = [[None] * 8 for _ in range(8)]
        inv = []
        for j in range(8):
            inv.append(1.0 / p[j][j])
            for i in range(j + 1, 8):
                l[i][j] = p[i][j] * inv[j]
            for i in range(j + 1, 8):
                for m in range(j + 1, i + 1):
                    p[i][m] = p[i][m] - l[i][j] * p[m][j]
        own = jnp.where(inside, jnp.where(lane - k == sub, 1.0, 0.0), w[b])
        rows = []
        for i in range(8):
            r = jnp.broadcast_to(own[i:i + 1], full)
            for j in range(i):
                r = r - l[i][j] * rows[j]
            rows.append(r)
        done = jnp.zeros(full, F32)
        for i in range(8):
            done = jnp.where(sub == i, rows[i] * (scale * lax.rsqrt(p[i][i])), done)
        out.append(jnp.where(lane < k + 8, done, 0.0))
        for rb in range(b + 1, RANK // 8):
            q = []
            new = jnp.where(inside, 0.0, w[rb])
            for j in range(8):
                v = jnp.broadcast_to(w[rb][:, k + j:k + j + 1], full)
                for i in range(j):
                    v = v - q[i] * l[j][i]
                q.append(v)
            for j in range(8):
                new = new - (q[j] * inv[j]) * rows[j]
            w[rb] = new
    return jnp.concatenate(out, axis=0)


def factor_kernel(scale, gram_hbm, st_hbm, cor_hbm, out_ref, cor_out, gram, st, w_ref, sem):
    loads = [pltpu.make_async_copy(gram_hbm, gram, sem.at[0]),
             pltpu.make_async_copy(st_hbm, st, sem.at[1]),
             pltpu.make_async_copy(cor_hbm, cor_out, sem.at[2])]
    for copy in loads:
        copy.start()
    loads[0].wait()
    w = [gram[8 * b:8 * b + 8] for b in range(RANK // 8)]
    w_ref[...] = inverse_factor(w, scale)
    loads[1].wait()
    out_ref[...] = lax.dot_general(st[...], w_ref[...], (((0,), (1,)), ((), ())),
                                   precision=lax.Precision.HIGHEST, preferred_element_type=F32)
    loads[2].wait()


def factor(gram, st, cor, scale):
    hbm = pl.BlockSpec(memory_space=pl.ANY)
    return pl.pallas_call(
        functools.partial(factor_kernel, scale),
        name="factor",
        out_shape=(jax.ShapeDtypeStruct((OWN, RANK), F32), jax.ShapeDtypeStruct(cor.shape, F32)),
        in_specs=[hbm, hbm, hbm],
        out_specs=(pl.BlockSpec(memory_space=pltpu.VMEM), hbm),
        scratch_shapes=[pltpu.VMEM((RANK, RANK), F32), pltpu.VMEM((RANK, OWN), F32), pltpu.VMEM((RANK, RANK), F32),
                        pltpu.SemaphoreType.DMA((3,))],
        compiler_params=pltpu.CompilerParams(vmem_limit_bytes=56 << 20),
    )(gram, st, cor)


def on_device(state, range_test, corange_test):
    total_cells = state.shape[1] * NC
    st, gram, corange = gather(state, range_test, corange_test)
    return factor(gram, st, corange, float(total_cells) ** 0.5)


def solution(mesh):
    return jax.shard_map(
        on_device,
        mesh=mesh,
        in_specs=(P("tm", "cell"), P("tm", None), P(None, "cell")),
        out_specs=(P(("cell", "tm"), None), P(None, "tm")),
        check_vma=False,
    )
```

```python
import functools

import jax
import jax.numpy as jnp
from jax import lax
from jax.experimental import pallas as pl
from jax.experimental.pallas import tpu as pltpu
from jax.sharding import PartitionSpec as P

MESH = pl.DeviceIdType.MESH
F32, BF16 = jnp.float32, jnp.bfloat16
NY, NZ, NC = 4, 8, 8
RANK, STEPS, OWN, HALF = 128, 256, 512, 256
A = 80
SCALE = 32768.0
ORDER = (4, 3, 5, 2, 6, 1, 7, 0)
FAR_C = (4, 5, 3, 2, 6, 7, 1)

GROUPS = ((0, 1), (1, 2), (3, 2), (5, 2), (7, 1))
PLUS, MINUS = 0, 1
SCHEDULE = (
    ("g", 0), ("s", 0), ("g", 1), ("g", 2), ("s", 1), ("c", 0), ("g", 3), ("c", 1), ("c", 2), ("b3", 0),
    ("a", 0), ("g", 4), ("s", 2), ("b2", 1), ("c", 3), ("g", 5), ("a", 1), ("b2", 0), ("c", 4), ("y", 0),
    ("g", 6), ("b1", 1), ("c", 5), ("s", 3), ("c", 6), ("a", 2), ("g", 7), ("b1", 0), ("c", 7), ("cs",),
    ("y", 1), ("A3",), ("s", 4), ("a", 3), ("b0",), ("y", 2), ("A2",), ("cq",), ("r",), ("a", 4), ("y", 3),
    ("A1",), ("q",), ("y", 4),
)


def encode(x):
    s = x * x
    return (s * x * jnp.abs(x)).astype(BF16)


def decode(y):
    y = y.astype(F32)
    r = lax.rsqrt(lax.rsqrt(jnp.maximum(jnp.abs(y), 1.2e-38)))
    return jnp.where(y < 0, -r, r)


def span(h):
    return pl.ds(h * HALF, HALF)


def gather_kernel(state_hbm, r_ref, c_hbm, st_out, gram_out, cor_out,
                  rt, sbuf, cbuf, part, cor,
                  sraw, rraw, sacc, racc, sz, rz, sb, rb, sraw2, rraw2, sacc2, racc2, crecv, cfull,
                  st, gpart, g1, g2, g3, g4,
                  load_sem, sem_raw, sem_acc, sem_z, sem_b, sem_raw2, sem_acc2,
                  sc, rc, sg1, rg1, sg2, rg2, sg3, rg3, sg4, rg4, out_sem):
    c, t = lax.axis_index("cell"), lax.axis_index("tm")
    y, z = t // NZ, lax.rem(t, NZ)

    def at_y(o):
        return (c, lax.rem(y + o, NY) * NZ + z)

    def at_z(o):
        return (c, y * NZ + lax.rem(z + o, NZ))

    def at_c(o):
        return (lax.rem(c + o, NC), t)

    barrier = pltpu.get_barrier_semaphore()
    peers = [at_y(o) for o in range(1, NY)] + [at_z(o) for o in range(1, NZ)] + [at_c(o) for o in range(1, NC)]
    for p in peers:
        pl.semaphore_signal(barrier, inc=1, device_id=p, device_id_type=MESH)

    def load(hbm, buf, i, yo):
        cols = pl.ds(pl.multiple_of(lax.rem(y + yo, NY) * (NZ * OWN), NZ * OWN), NZ * OWN)
        return pltpu.make_async_copy(hbm.at[:, cols], buf.at[yo], load_sem.at[i, yo])

    for yo in range(NY):
        load(state_hbm, sbuf, 0, yo).start()
    for yo in range(NY):
        load(c_hbm, cbuf, 1, yo).start()

    rt[...] = (r_ref[...].astype(F32) * SCALE).T.astype(BF16)

    to_y = (at_y(1), at_y(NY - 1))
    to_z = (at_z(1), at_z(NZ - 1))
    pending = []

    def message(src, dst, sems, i, to):
        return pltpu.make_async_remote_copy(
            src, dst, sems.at[(0,) + i], sems.at[(1,) + i], device_id=to, device_id_type=MESH)

    def send(copy):
        copy.start()
        pending.append(copy)

    def lanes(zo):
        return pl.ds(pl.multiple_of(lax.rem(z + zo, NZ) * OWN, OWN), OWN)

    def multiply(p):
        zo = ORDER[p]

        @pl.loop(0, NY)
        def _(yo):
            part[zo, yo] = jnp.dot(rt[...], sbuf[yo, :, lanes(zo)], preferred_element_type=F32)

    def pa(zo, yo, h):
        return part[zo, yo, 0:A, span(h)]

    def pb(zo, yo, h):
        return part[zo, yo, A:RANK, span(h)]

    def raw_y(d, put, own):
        put(0, encode(own(2, d)))
        put(1, encode(own(1 if d == PLUS else 3, 1 - d)))

    def a_raw(g, d):
        at = pl.ds(*GROUPS[g])
        return message(sraw.at[d, at], rraw.at[d, at], sem_raw, (d, g), to_y[d])

    def a_acc(g, d):
        at = pl.ds(*GROUPS[g])
        return message(sacc.at[d, at], racc.at[d, at], sem_acc, (d, g), to_y[d])

    def positions(g):
        return range(GROUPS[g][0], GROUPS[g][0] + GROUPS[g][1])

    def sends(g):
        for d in (PLUS, MINUS):
            for p in positions(g):
                def put(slot, value):
                    sraw[d, p, slot] = value

                raw_y(d, put, lambda yo, h: pa(ORDER[p], yo, h))
            send(a_raw(g, d))

    def acc(g):
        for d in (PLUS, MINUS):
            a_raw(g, d).wait_recv()
            for p in positions(g):
                own = pa(ORDER[p], 1 if d == PLUS else 3, d)
                sacc[d, p] = encode(own + decode(rraw[d, p, 0]))
            send(a_acc(g, d))

    def z_msg(d, k):
        src, dst = (sz.at[d, 0, 0], rz.at[d, 0, 0]) if k == 4 else (sz.at[d, 4 - k], rz.at[d, 4 - k])
        return message(src, dst, sem_z, (d, 4 - k), to_z[d])

    def toward(d, k):
        return k if d == PLUS else NZ - k

    def z_far():
        for d in (PLUS, MINUS):
            sz[d, 0, 0] = encode(pa(4, 0, d))
            send(z_msg(d, 4))

    def z_step(k):
        for d in (PLUS, MINUS):
            zo = toward(d, k)
            z_msg(d, k + 1).wait_recv()
            sz[d, 4 - k, 0] = encode(pa(zo, 0, d) + decode(rz[d, 3 - k, 0]))
            other = pa(zo, 0, 1 - d)
            sz[d, 4 - k, 1] = encode(other if k == 3 else other + decode(rz[d, 3 - k, 1]))
            send(z_msg(d, k))

    def y_done(g):
        for d in (PLUS, MINUS):
            a_acc(g, d).wait_recv()
        for p in positions(g):
            zo = ORDER[p]
            for h in (0, 1):
                part[zo, 0, 0:A, span(h)] = pa(zo, 0, h) + decode(rraw[1 - h, p, 1]) + decode(racc[h, p])
        if g == 0:
            z_far()

    def b_msg(d, k, chain):
        i = (d, 4 - k, chain)
        return message(sb.at[i], rb.at[i], sem_b, i, to_z[d])

    def b_raw(d, k, chain):
        for yo in range(NY):
            sb[d, 4 - k, chain, yo] = encode(pb(toward(d, k), yo, d if chain == 0 else 1 - d))
        send(b_msg(d, k, chain))

    def b_step(k):
        def go(chain):
            for d in (PLUS, MINUS):
                b_msg(d, k + 1, chain).wait_recv()
                for yo in range(NY):
                    own = pb(toward(d, k), yo, d if chain == 0 else 1 - d)
                    sb[d, 4 - k, chain, yo] = encode(own + decode(rb[d, 3 - k, chain, yo]))
                send(b_msg(d, k, chain))

        return go

    def b_done():
        for d in (PLUS, MINUS):
            for chain in (0, 1):
                b_msg(d, 1, chain).wait_recv()
        for yo in range(NY):
            for h in (0, 1):
                part[0, yo, A:RANK, span(h)] = (
                    pb(0, yo, h) + decode(rb[h, 3, 0, yo]) + decode(rb[1 - h, 3, 1, yo]))

    def r_msg(d):
        return message(sraw2.at[d], rraw2.at[d], sem_raw2, (d,), to_y[d])

    def q_msg(d):
        return message(sacc2.at[d], racc2.at[d], sem_acc2, (d,), to_y[d])

    def raw2():
        for d in (PLUS, MINUS):
            def put(slot, value):
                sraw2[d, slot] = value

            raw_y(d, put, lambda yo, h: pb(0, yo, h))
            send(r_msg(d))

    def acc2():
        for d in (PLUS, MINUS):
            r_msg(d).wait_recv()
            sacc2[d] = encode(pb(0, 1 if d == PLUS else 3, d) + decode(rraw2[d, 0]))
            send(q_msg(d))

    def group(p):
        if p == 0:
            for yo in range(NY):
                load(state_hbm, sbuf, 0, yo).wait()
        multiply(p)
        if p == 0:
            pl.semaphore_wait(barrier, len(peers))
            b_raw(PLUS, 4, 0)
            b_raw(MINUS, 4, 0)
        if p in (1, 2):
            b_raw(p - 1, 3, 1)

    cor[...] = jnp.zeros_like(cor)

    def correlate(p):
        zo = ORDER[p]
        if p == 0:
            for yo in range(NY):
                load(c_hbm, cbuf, 1, yo).wait()

        @pl.loop(0, NY)
        def _(yo):
            cor[...] += lax.dot_general(
                cbuf[yo, :, lanes(zo)], sbuf[yo, :, lanes(zo)], (((1,), (1,)), ((), ())), preferred_element_type=F32
            )

    rows = 256 // NC

    def strip(i, n):
        return pl.ds(pl.multiple_of(i * n, n), n)

    def near_c(o):
        return lax.rem(c + o, NC)

    def cor_rs(o):
        return pltpu.make_async_remote_copy(
            cor.at[strip(near_c(o), rows)], crecv.at[o - 1], sc.at[0, o - 1], rc.at[0, o - 1],
            device_id=at_c(o), device_id_type=MESH)

    def cor_ag(o, owner):
        return pltpu.make_async_remote_copy(
            cfull.at[strip(owner, rows)], cfull.at[strip(owner, rows)], sc.at[1, o - 1], rc.at[1, owner],
            device_id=at_c(o), device_id_type=MESH)

    def cor_send():
        for o in FAR_C:
            cor_rs(o).start()

    def cor_sum():
        total = cor[strip(c, rows)]
        for o in range(1, NC):
            cor_rs(o).wait_recv()
            total = total + crecv[o - 1]
        cfull[strip(c, rows)] = total
        for o in FAR_C:
            cor_ag(o, c).start()

    acts = {
        "g": group, "s": sends, "a": acc, "y": y_done, "c": correlate, "cs": cor_send, "cq": cor_sum,
        "b3": b_step(3), "b2": b_step(2), "b1": b_step(1), "b0": b_done,
        "A3": lambda: z_step(3), "A2": lambda: z_step(2), "A1": lambda: z_step(1), "r": raw2, "q": acc2,
    }
    for act, *which in SCHEDULE:
        acts[act](*which)

    for d in (PLUS, MINUS):
        q_msg(d).wait_recv()
    for h in (0, 1):
        st[A:RANK, span(h)] = pb(0, 0, h) + decode(rraw2[1 - h, 1]) + decode(racc2[h])
    for d in (PLUS, MINUS):
        z_msg(d, 1).wait_recv()
    for h in (0, 1):
        st[0:A, span(h)] = pa(0, 0, h) + decode(rz[h, 3, 0]) + decode(rz[1 - h, 3, 1])

    sk = st[...]
    gpart[...] = lax.dot_general(sk, sk, (((1,), (1,)), ((), ())),
                                 precision=lax.Precision.HIGHEST, preferred_element_type=F32)
    gr = RANK // NC

    def rs1(o):
        return pltpu.make_async_remote_copy(
            gpart.at[strip(near_c(o), gr)], g1.at[o - 1], sg1.at[o - 1], rg1.at[o - 1],
            device_id=at_c(o), device_id_type=MESH)

    def ag2(o, owner):
        return pltpu.make_async_remote_copy(
            g2.at[owner], g2.at[owner], sg2.at[o - 1], rg2.at[owner], device_id=at_y(o), device_id_type=MESH)

    def ag3(o, owner):
        return pltpu.make_async_remote_copy(
            g3.at[owner], g3.at[owner], sg3.at[o - 1], rg3.at[owner], device_id=at_z(o), device_id_type=MESH)

    def ag4(o, owner):
        return pltpu.make_async_remote_copy(
            g4.at[strip(owner, gr)], g4.at[strip(owner, gr)], sg4.at[o - 1], rg4.at[owner],
            device_id=at_c(o), device_id_type=MESH)

    for o in FAR_C:
        rs1(o).start()
    outs = [pltpu.make_async_copy(st, st_out, out_sem.at[0]),
            pltpu.make_async_copy(cfull, cor_out, out_sem.at[1]),
            pltpu.make_async_copy(g4, gram_out, out_sem.at[2])]
    outs[0].start()
    total = gpart[strip(c, gr)]
    for o in FAR_C[::-1]:
        rs1(o).wait_recv()
        total = total + g1[o - 1]
    g2[y] = total
    for o in (2, 1, 3):
        ag2(o, y).start()
    for o in range(1, NC):
        cor_ag(o, near_c(o)).wait_recv()
    outs[1].start()
    for o in (1, 3, 2):
        ag2(o, lax.rem(y + o, NY)).wait_recv()
    total = g2[0]
    for i in range(1, NY):
        total = total + g2[i]
    g3[z] = total
    for o in (4, 3, 5, 2, 6, 1, 7):
        ag3(o, z).start()
    for copy in pending:
        copy.wait_send()
    for o in range(1, NC):
        cor_rs(o).wait_send()
        cor_ag(o, c).wait_send()
        rs1(o).wait_send()
    for o in range(1, NY):
        ag2(o, y).wait_send()
    for o in (1, 7, 2, 6, 3, 5, 4):
        ag3(o, lax.rem(z + o, NZ)).wait_recv()
    total = g3[0]
    for i in range(1, NZ):
        total = total + g3[i]
    g4[strip(c, gr)] = total
    for o in FAR_C:
        ag4(o, c).start()
    for o in range(1, NZ):
        ag3(o, z).wait_send()
    outs[0].wait()
    outs[1].wait()
    for o in FAR_C[::-1]:
        ag4(o, near_c(o)).wait_recv()
    outs[2].start()
    for o in range(1, NC):
        ag4(o, c).wait_send()
    outs[2].wait()


def gather(state, range_test, corange_test):
    dma = pltpu.SemaphoreType.DMA
    B = RANK - A

    def bf(*s):
        return pltpu.VMEM(s, BF16)

    def fl(*s):
        return pltpu.VMEM(s, F32)

    vmem = pl.BlockSpec(memory_space=pltpu.VMEM)
    hbm = pl.BlockSpec(memory_space=pl.ANY)
    return pl.pallas_call(
        gather_kernel,
        name="sketch_sums",
        out_shape=(
            jax.ShapeDtypeStruct((RANK, OWN), F32),
            jax.ShapeDtypeStruct((RANK, RANK), F32),
            jax.ShapeDtypeStruct((256, 256), F32),
        ),
        in_specs=[hbm, vmem, hbm],
        out_specs=(hbm, hbm, hbm),
        scratch_shapes=[
            bf(RANK, STEPS), bf(NY, STEPS, NZ * OWN), bf(NY, 256, NZ * OWN), fl(NZ, NY, RANK, OWN), fl(256, 256),
            bf(2, NZ, 2, A, HALF), bf(2, NZ, 2, A, HALF), bf(2, NZ, A, HALF), bf(2, NZ, A, HALF),
            bf(2, 4, 2, A, HALF), bf(2, 4, 2, A, HALF), bf(2, 4, 2, NY, B, HALF), bf(2, 4, 2, NY, B, HALF),
            bf(2, 2, B, HALF), bf(2, 2, B, HALF), bf(2, B, HALF), bf(2, B, HALF),
            fl(7, 32, 256), fl(256, 256),
            fl(RANK, OWN), fl(RANK, RANK), fl(7, 16, RANK), fl(NY, 16, RANK), fl(NZ, 16, RANK), fl(RANK, RANK),
            dma((2, NY)), dma((2, 2, 5)), dma((2, 2, 5)), dma((2, 2, 4)), dma((2, 2, 4, 2)), dma((2, 2)), dma((2, 2)),
            dma((2, 7)), dma((2, NC)),
            dma((7,)), dma((7,)), dma((3,)), dma((NY,)), dma((7,)), dma((NZ,)), dma((7,)), dma((NC,)), dma((3,)),
        ],
        compiler_params=pltpu.CompilerParams(
            collective_id=1, has_side_effects=True, vmem_limit_bytes=56 << 20),
    )(state, range_test, corange_test)


def inverse_factor(w, scale, midway):
    lane = lax.broadcasted_iota(jnp.int32, (8, RANK), 1)
    sub = lax.broadcasted_iota(jnp.int32, (8, RANK), 0)
    full = (8, RANK)
    out = []
    for b in range(RANK // 8):
        k = 8 * b
        if b == 6:
            midway()
        inside = (lane >= k) & (lane < k + 8)
        cols = [jnp.broadcast_to(w[b][:, k + j:k + j + 1], full) for j in range(8)]
        p = [[jnp.broadcast_to(cols[j][i:i + 1], full) for j in range(i + 1)] for i in range(8)]
        l = [[None] * 8 for _ in range(8)]
        inv = []
        for j in range(8):
            inv.append(1.0 / p[j][j])
            for i in range(j + 1, 8):
                l[i][j] = p[i][j] * inv[j]
            for i in range(j + 1, 8):
                for m in range(j + 1, i + 1):
                    p[i][m] = p[i][m] - l[i][j] * p[m][j]
        own = jnp.where(inside, jnp.where(lane - k == sub, 1.0, 0.0), w[b])
        rows = []
        for i in range(8):
            r = jnp.broadcast_to(own[i:i + 1], full)
            for j in range(i):
                r = r - l[i][j] * rows[j]
            rows.append(r)
        done = jnp.zeros(full, F32)
        for i in range(8):
            done = jnp.where(sub == i, rows[i] * (scale * lax.rsqrt(p[i][i])), done)
        out.append(jnp.where(lane < k + 8, done, 0.0))
        for rb in range(b + 1, RANK // 8):
            q = []
            new = jnp.where(inside, 0.0, w[rb])
            for j in range(8):
                v = jnp.broadcast_to(w[rb][:, k + j:k + j + 1], full)
                for i in range(j):
                    v = v - q[i] * l[j][i]
                q.append(v)
            for j in range(8):
                new = new - (q[j] * inv[j]) * rows[j]
            w[rb] = new
    return jnp.concatenate(out, axis=0)


def factor_kernel(scale, gram_hbm, st_hbm, cor_hbm, out_ref, cor_out, gram, st, cor, w_ref, sem):
    loads = [pltpu.make_async_copy(gram_hbm, gram, sem.at[0]),
             pltpu.make_async_copy(cor_hbm, cor, sem.at[1]),
             pltpu.make_async_copy(st_hbm, st, sem.at[2])]
    for copy in loads:
        copy.start()
    store = pltpu.make_async_copy(cor, cor_out, sem.at[3])

    def midway():
        loads[1].wait()
        store.start()

    loads[0].wait()
    w = [gram[8 * b:8 * b + 8] for b in range(RANK // 8)]
    w_ref[...] = inverse_factor(w, scale, midway)
    loads[2].wait()
    out_ref[...] = lax.dot_general(st[...], w_ref[...], (((0,), (1,)), ((), ())),
                                   precision=lax.Precision.HIGHEST, preferred_element_type=F32)
    store.wait()


def factor(gram, st, cor, scale):
    hbm = pl.BlockSpec(memory_space=pl.ANY)
    return pl.pallas_call(
        functools.partial(factor_kernel, scale),
        name="factor",
        out_shape=(jax.ShapeDtypeStruct((OWN, RANK), F32), jax.ShapeDtypeStruct(cor.shape, F32)),
        in_specs=[hbm, hbm, hbm],
        out_specs=(pl.BlockSpec(memory_space=pltpu.VMEM), hbm),
        scratch_shapes=[pltpu.VMEM((RANK, RANK), F32), pltpu.VMEM((RANK, OWN), F32), pltpu.VMEM(cor.shape, F32),
                        pltpu.VMEM((RANK, RANK), F32), pltpu.SemaphoreType.DMA((4,))],
        compiler_params=pltpu.CompilerParams(vmem_limit_bytes=56 << 20),
    )(gram, st, cor)


def on_device(state, range_test, corange_test):
    total_cells = state.shape[1] * NC
    st, gram, corange = gather(state, range_test, corange_test)
    return factor(gram, st, corange, float(total_cells) ** 0.5)


def solution(mesh):
    return jax.shard_map(
        on_device,
        mesh=mesh,
        in_specs=(P("tm", "cell"), P("tm", None), P(None, "cell")),
        out_specs=(P(("cell", "tm"), None), P(None, "tm")),
        check_vma=False,
    )
```

```python
import functools

import jax
import jax.numpy as jnp
from jax import lax
from jax.experimental import pallas as pl
from jax.experimental.pallas import tpu as pltpu
from jax.sharding import PartitionSpec as P

MESH = pl.DeviceIdType.MESH
F32, BF16 = jnp.float32, jnp.bfloat16
NY, NZ, NC = 4, 8, 8
RANK, STEPS, OWN, HALF = 128, 256, 512, 256
A = 80
SCALE = 32768.0
ORDER = (4, 3, 5, 2, 6, 1, 7, 0)
FAR_C = (4, 5, 3, 2, 6, 7, 1)

GROUPS = ((0, 1), (1, 2), (3, 2), (5, 2), (7, 1))
PLUS, MINUS = 0, 1
SCHEDULE = (
    ("g", 0), ("s", 0), ("g", 1), ("g", 2), ("s", 1), ("g", 3), ("c", 0), ("g", 4), ("c", 1), ("b3", 0),
    ("a", 0), ("s", 2), ("g", 5), ("g", 6), ("c", 2), ("b2", 1), ("a", 1), ("c", 3), ("c", 4), ("y", 0),
    ("g", 7), ("b2", 0), ("c", 5), ("s", 3), ("c", 6), ("b1", 1), ("c", 7), ("cs",), ("y", 1), ("A3",),
    ("a", 2), ("b1", 0), ("s", 4), ("a", 3), ("y", 2), ("A2",), ("cq",), ("b0",), ("r",), ("a", 4), ("y", 3),
    ("A1",), ("q",), ("y", 4),
)


def encode(x):
    s = x * x
    return (s * x * jnp.abs(x)).astype(BF16)


def decode(y):
    y = y.astype(F32)
    r = lax.rsqrt(lax.rsqrt(jnp.maximum(jnp.abs(y), 1.2e-38)))
    return jnp.where(y < 0, -r, r)


def span(h):
    return pl.ds(h * HALF, HALF)


def gather_kernel(state_hbm, r_hbm, c_hbm, st_out, gram_out, cor_out,
                  rbuf, rt, sbuf, cbuf, part, cor,
                  sraw, rraw, sacc, racc, sz, rz, sb, rb, sraw2, rraw2, sacc2, racc2, crecv, cfull,
                  st, gpart, g1, g2, g3, g4,
                  load_sem, sem_raw, sem_acc, sem_z, sem_b, sem_raw2, sem_acc2,
                  sc, rc, sg1, rg1, sg2, rg2, sg3, rg3, sg4, rg4, out_sem):
    c, t = lax.axis_index("cell"), lax.axis_index("tm")
    y, z = t // NZ, lax.rem(t, NZ)

    def at_y(o):
        return (c, lax.rem(y + o, NY) * NZ + z)

    def at_z(o):
        return (c, y * NZ + lax.rem(z + o, NZ))

    def at_c(o):
        return (lax.rem(c + o, NC), t)

    barrier = pltpu.get_barrier_semaphore()
    peers = [at_y(o) for o in range(1, NY)] + [at_z(o) for o in range(1, NZ)] + [at_c(o) for o in range(1, NC)]
    for p in peers:
        pl.semaphore_signal(barrier, inc=1, device_id=p, device_id_type=MESH)

    def load(hbm, buf, i, yo):
        cols = pl.ds(pl.multiple_of(lax.rem(y + yo, NY) * (NZ * OWN), NZ * OWN), NZ * OWN)
        return pltpu.make_async_copy(hbm.at[:, cols], buf.at[yo], load_sem.at[i, yo])

    load_r = pltpu.make_async_copy(r_hbm, rbuf, out_sem.at[3])
    load_r.start()
    for yo in range(NY):
        load(state_hbm, sbuf, 0, yo).start()
    for yo in range(NY):
        load(c_hbm, cbuf, 1, yo).start()

    load_r.wait()
    rt[...] = (rbuf[...].astype(F32) * SCALE).T.astype(BF16)

    to_y = (at_y(1), at_y(NY - 1))
    to_z = (at_z(1), at_z(NZ - 1))
    pending = []

    def message(src, dst, sems, i, to):
        return pltpu.make_async_remote_copy(
            src, dst, sems.at[(0,) + i], sems.at[(1,) + i], device_id=to, device_id_type=MESH)

    def send(copy):
        copy.start()
        pending.append(copy)

    def lanes(zo):
        return pl.ds(pl.multiple_of(lax.rem(z + zo, NZ) * OWN, OWN), OWN)

    def multiply(p):
        zo = ORDER[p]

        @pl.loop(0, NY)
        def _(yo):
            part[zo, yo] = jnp.dot(rt[...], sbuf[yo, :, lanes(zo)], preferred_element_type=F32)

    def pa(zo, yo, h):
        return part[zo, yo, 0:A, span(h)]

    def pb(zo, yo, h):
        return part[zo, yo, A:RANK, span(h)]

    def raw_y(d, put, own):
        put(0, encode(own(2, d)))
        put(1, encode(own(1 if d == PLUS else 3, 1 - d)))

    def a_raw(g, d):
        at = pl.ds(*GROUPS[g])
        return message(sraw.at[d, at], rraw.at[d, at], sem_raw, (d, g), to_y[d])

    def a_acc(g, d):
        at = pl.ds(*GROUPS[g])
        return message(sacc.at[d, at], racc.at[d, at], sem_acc, (d, g), to_y[d])

    def positions(g):
        return range(GROUPS[g][0], GROUPS[g][0] + GROUPS[g][1])

    def sends(g):
        for d in (PLUS, MINUS):
            for p in positions(g):
                def put(slot, value):
                    sraw[d, p, slot] = value

                raw_y(d, put, lambda yo, h: pa(ORDER[p], yo, h))
            send(a_raw(g, d))

    def acc(g):
        for d in (PLUS, MINUS):
            a_raw(g, d).wait_recv()
            for p in positions(g):
                own = pa(ORDER[p], 1 if d == PLUS else 3, d)
                sacc[d, p] = encode(own + decode(rraw[d, p, 0]))
            send(a_acc(g, d))

    def z_msg(d, k):
        src, dst = (sz.at[d, 0, 0], rz.at[d, 0, 0]) if k == 4 else (sz.at[d, 4 - k], rz.at[d, 4 - k])
        return message(src, dst, sem_z, (d, 4 - k), to_z[d])

    def toward(d, k):
        return k if d == PLUS else NZ - k

    def z_far():
        for d in (PLUS, MINUS):
            sz[d, 0, 0] = encode(pa(4, 0, d))
            send(z_msg(d, 4))

    def z_step(k):
        for d in (PLUS, MINUS):
            zo = toward(d, k)
            z_msg(d, k + 1).wait_recv()
            sz[d, 4 - k, 0] = encode(pa(zo, 0, d) + decode(rz[d, 3 - k, 0]))
            other = pa(zo, 0, 1 - d)
            sz[d, 4 - k, 1] = encode(other if k == 3 else other + decode(rz[d, 3 - k, 1]))
            send(z_msg(d, k))

    def y_done(g):
        for d in (PLUS, MINUS):
            a_acc(g, d).wait_recv()
        for p in positions(g):
            zo = ORDER[p]
            for h in (0, 1):
                part[zo, 0, 0:A, span(h)] = pa(zo, 0, h) + decode(rraw[1 - h, p, 1]) + decode(racc[h, p])
        if g == 0:
            z_far()

    def b_msg(d, k, chain):
        i = (d, 4 - k, chain)
        return message(sb.at[i], rb.at[i], sem_b, i, to_z[d])

    def b_raw(d, k, chain):
        for yo in range(NY):
            sb[d, 4 - k, chain, yo] = encode(pb(toward(d, k), yo, d if chain == 0 else 1 - d))
        send(b_msg(d, k, chain))

    def b_step(k):
        def go(chain):
            for d in (PLUS, MINUS):
                b_msg(d, k + 1, chain).wait_recv()
                for yo in range(NY):
                    own = pb(toward(d, k), yo, d if chain == 0 else 1 - d)
                    sb[d, 4 - k, chain, yo] = encode(own + decode(rb[d, 3 - k, chain, yo]))
                send(b_msg(d, k, chain))

        return go

    def b_done():
        for d in (PLUS, MINUS):
            for chain in (0, 1):
                b_msg(d, 1, chain).wait_recv()
        for yo in range(NY):
            for h in (0, 1):
                part[0, yo, A:RANK, span(h)] = (
                    pb(0, yo, h) + decode(rb[h, 3, 0, yo]) + decode(rb[1 - h, 3, 1, yo]))

    def r_msg(d):
        return message(sraw2.at[d], rraw2.at[d], sem_raw2, (d,), to_y[d])

    def q_msg(d):
        return message(sacc2.at[d], racc2.at[d], sem_acc2, (d,), to_y[d])

    def raw2():
        for d in (PLUS, MINUS):
            def put(slot, value):
                sraw2[d, slot] = value

            raw_y(d, put, lambda yo, h: pb(0, yo, h))
            send(r_msg(d))

    def acc2():
        for d in (PLUS, MINUS):
            r_msg(d).wait_recv()
            sacc2[d] = encode(pb(0, 1 if d == PLUS else 3, d) + decode(rraw2[d, 0]))
            send(q_msg(d))

    def group(p):
        if p == 0:
            for yo in range(NY):
                load(state_hbm, sbuf, 0, yo).wait()
        multiply(p)
        if p == 0:
            pl.semaphore_wait(barrier, len(peers))
            b_raw(PLUS, 4, 0)
            b_raw(MINUS, 4, 0)
        if p in (1, 2):
            b_raw(p - 1, 3, 1)

    wide = NZ * OWN // 2

    def correlate(i):
        if i == 0:
            for yo in range(NY):
                load(c_hbm, cbuf, 1, yo).wait()
        cols = pl.ds(i % 2 * wide, wide)
        product = lax.dot_general(
            cbuf[i // 2, :, cols], sbuf[i // 2, :, cols], (((1,), (1,)), ((), ())), preferred_element_type=F32)
        cor[...] = product if i == 0 else cor[...] + product

    rows = 256 // NC

    def strip(i, n):
        return pl.ds(pl.multiple_of(i * n, n), n)

    def near_c(o):
        return lax.rem(c + o, NC)

    def cor_rs(o):
        return pltpu.make_async_remote_copy(
            cor.at[strip(near_c(o), rows)], crecv.at[o - 1], sc.at[0, o - 1], rc.at[0, o - 1],
            device_id=at_c(o), device_id_type=MESH)

    def cor_ag(o, owner):
        return pltpu.make_async_remote_copy(
            cfull.at[strip(owner, rows)], cfull.at[strip(owner, rows)], sc.at[1, o - 1], rc.at[1, owner],
            device_id=at_c(o), device_id_type=MESH)

    def cor_send():
        for o in FAR_C:
            cor_rs(o).start()

    def cor_sum():
        total = cor[strip(c, rows)]
        for o in range(1, NC):
            cor_rs(o).wait_recv()
            total = total + crecv[o - 1]
        cfull[strip(c, rows)] = total
        for o in FAR_C:
            cor_ag(o, c).start()

    acts = {
        "g": group, "s": sends, "a": acc, "y": y_done, "c": correlate, "cs": cor_send, "cq": cor_sum,
        "b3": b_step(3), "b2": b_step(2), "b1": b_step(1), "b0": b_done,
        "A3": lambda: z_step(3), "A2": lambda: z_step(2), "A1": lambda: z_step(1), "r": raw2, "q": acc2,
    }
    for act, *which in SCHEDULE:
        acts[act](*which)

    for d in (PLUS, MINUS):
        q_msg(d).wait_recv()
    for h in (0, 1):
        st[A:RANK, span(h)] = pb(0, 0, h) + decode(rraw2[1 - h, 1]) + decode(racc2[h])
    for d in (PLUS, MINUS):
        z_msg(d, 1).wait_recv()
    for h in (0, 1):
        st[0:A, span(h)] = pa(0, 0, h) + decode(rz[h, 3, 0]) + decode(rz[1 - h, 3, 1])

    sk = st[...]
    st_out[...] = sk
    gpart[...] = lax.dot_general(sk, sk, (((1,), (1,)), ((), ())),
                                 precision=lax.Precision.HIGHEST, preferred_element_type=F32)
    gr = RANK // NC

    def rs1(o):
        return pltpu.make_async_remote_copy(
            gpart.at[strip(near_c(o), gr)], g1.at[o - 1], sg1.at[o - 1], rg1.at[o - 1],
            device_id=at_c(o), device_id_type=MESH)

    def ag2(o, owner):
        return pltpu.make_async_remote_copy(
            g2.at[owner], g2.at[owner], sg2.at[o - 1], rg2.at[owner], device_id=at_y(o), device_id_type=MESH)

    def ag3(o, owner):
        return pltpu.make_async_remote_copy(
            g3.at[owner], g3.at[owner], sg3.at[o - 1], rg3.at[owner], device_id=at_z(o), device_id_type=MESH)

    def ag4(o, owner):
        return pltpu.make_async_remote_copy(
            g4.at[strip(owner, gr)], g4.at[strip(owner, gr)], sg4.at[o - 1], rg4.at[owner],
            device_id=at_c(o), device_id_type=MESH)

    for o in FAR_C:
        rs1(o).start()
    total = gpart[strip(c, gr)]
    for o in FAR_C[::-1]:
        rs1(o).wait_recv()
        total = total + g1[o - 1]
    g2[y] = total
    for o in (2, 1, 3):
        ag2(o, y).start()
    for o in range(1, NC):
        cor_ag(o, near_c(o)).wait_recv()
    cor_out[...] = cfull[...]
    for o in (1, 3, 2):
        ag2(o, lax.rem(y + o, NY)).wait_recv()
    total = g2[0]
    for i in range(1, NY):
        total = total + g2[i]
    g3[z] = total
    for o in (4, 3, 5, 2, 6, 1, 7):
        ag3(o, z).start()
    for copy in pending:
        copy.wait_send()
    for o in range(1, NC):
        cor_rs(o).wait_send()
        cor_ag(o, c).wait_send()
        rs1(o).wait_send()
    for o in range(1, NY):
        ag2(o, y).wait_send()
    for o in (1, 7, 2, 6, 3, 5, 4):
        ag3(o, lax.rem(z + o, NZ)).wait_recv()
    total = g3[0]
    for i in range(1, NZ):
        total = total + g3[i]
    g4[strip(c, gr)] = total
    for o in FAR_C:
        ag4(o, c).start()
    for o in range(1, NZ):
        ag3(o, z).wait_send()
    for o in FAR_C[::-1]:
        ag4(o, near_c(o)).wait_recv()
    gram_out[...] = g4[...]
    for o in range(1, NC):
        ag4(o, c).wait_send()


def gather(state, range_test, corange_test):
    dma = pltpu.SemaphoreType.DMA
    B = RANK - A

    def bf(*s):
        return pltpu.VMEM(s, BF16)

    def fl(*s):
        return pltpu.VMEM(s, F32)

    vmem = pl.BlockSpec(memory_space=pltpu.VMEM)
    hbm = pl.BlockSpec(memory_space=pl.ANY)
    return pl.pallas_call(
        gather_kernel,
        name="sketch_sums",
        out_shape=(pltpu.VMEM((RANK, OWN), F32), pltpu.VMEM((RANK, RANK), F32), pltpu.VMEM((256, 256), F32)),
        in_specs=[hbm, hbm, hbm],
        out_specs=(vmem, vmem, vmem),
        scratch_shapes=[
            bf(STEPS, RANK), bf(RANK, STEPS), bf(NY, STEPS, NZ * OWN), bf(NY, 256, NZ * OWN), fl(NZ, NY, RANK, OWN), fl(256, 256),
            bf(2, NZ, 2, A, HALF), bf(2, NZ, 2, A, HALF), bf(2, NZ, A, HALF), bf(2, NZ, A, HALF),
            bf(2, 4, 2, A, HALF), bf(2, 4, 2, A, HALF), bf(2, 4, 2, NY, B, HALF), bf(2, 4, 2, NY, B, HALF),
            bf(2, 2, B, HALF), bf(2, 2, B, HALF), bf(2, B, HALF), bf(2, B, HALF),
            fl(7, 32, 256), fl(256, 256),
            fl(RANK, OWN), fl(RANK, RANK), fl(7, 16, RANK), fl(NY, 16, RANK), fl(NZ, 16, RANK), fl(RANK, RANK),
            dma((2, NY)), dma((2, 2, 5)), dma((2, 2, 5)), dma((2, 2, 4)), dma((2, 2, 4, 2)), dma((2, 2)), dma((2, 2)),
            dma((2, 7)), dma((2, NC)),
            dma((7,)), dma((7,)), dma((3,)), dma((NY,)), dma((7,)), dma((NZ,)), dma((7,)), dma((NC,)), dma((4,)),
        ],
        compiler_params=pltpu.CompilerParams(
            collective_id=1, has_side_effects=True, vmem_limit_bytes=60 << 20),
    )(state, range_test, corange_test)


def inverse_factor(w, scale):
    lane = lax.broadcasted_iota(jnp.int32, (8, RANK), 1)
    sub = lax.broadcasted_iota(jnp.int32, (8, RANK), 0)
    full = (8, RANK)
    out = []
    for b in range(RANK // 8):
        k = 8 * b
        inside = (lane >= k) & (lane < k + 8)
        cols = [jnp.broadcast_to(w[b][:, k + j:k + j + 1], full) for j in range(8)]
        p = [[jnp.broadcast_to(cols[j][i:i + 1], full) for j in range(i + 1)] for i in range(8)]
        l = [[None] * 8 for _ in range(8)]
        inv = []
        for j in range(8):
            inv.append(1.0 / p[j][j])
            for i in range(j + 1, 8):
                l[i][j] = p[i][j] * inv[j]
            for i in range(j + 1, 8):
                for m in range(j + 1, i + 1):
                    p[i][m] = p[i][m] - l[i][j] * p[m][j]
        own = jnp.where(inside, jnp.where(lane - k == sub, 1.0, 0.0), w[b])
        rows = []
        for i in range(8):
            r = jnp.broadcast_to(own[i:i + 1], full)
            for j in range(i):
                r = r - l[i][j] * rows[j]
            rows.append(r)
        done = jnp.zeros(full, F32)
        for i in range(8):
            done = jnp.where(sub == i, rows[i] * (scale * lax.rsqrt(p[i][i])), done)
        out.append(jnp.where(lane < k + 8, done, 0.0))
        for rb in range(b + 1, RANK // 8):
            q = []
            new = jnp.where(inside, 0.0, w[rb])
            for j in range(8):
                v = jnp.broadcast_to(w[rb][:, k + j:k + j + 1], full)
                for i in range(j):
                    v = v - q[i] * l[j][i]
                q.append(v)
            for j in range(8):
                new = new - (q[j] * inv[j]) * rows[j]
            w[rb] = new
    return jnp.concatenate(out, axis=0)


def factor_kernel(scale, gram, st, cor, out_hbm, cor_out, basis, w_ref, sem):
    store = pltpu.make_async_copy(cor, cor_out, sem.at[0])
    store.start()
    w = [gram[8 * b:8 * b + 8] for b in range(RANK // 8)]
    w_ref[...] = inverse_factor(w, scale)
    basis[...] = lax.dot_general(st[...], w_ref[...], (((0,), (1,)), ((), ())),
                                 precision=lax.Precision.HIGHEST, preferred_element_type=F32)
    out = pltpu.make_async_copy(basis, out_hbm, sem.at[1])
    out.start()
    store.wait()
    out.wait()


def factor(gram, st, cor, scale):
    hbm = pl.BlockSpec(memory_space=pl.ANY)
    vmem = pl.BlockSpec(memory_space=pltpu.VMEM)
    return pl.pallas_call(
        functools.partial(factor_kernel, scale),
        name="factor",
        out_shape=(jax.ShapeDtypeStruct((OWN, RANK), F32), jax.ShapeDtypeStruct(cor.shape, F32)),
        in_specs=[vmem, vmem, vmem],
        out_specs=(hbm, hbm),
        scratch_shapes=[pltpu.VMEM((OWN, RANK), F32), pltpu.VMEM((RANK, RANK), F32), pltpu.SemaphoreType.DMA((2,))],
        compiler_params=pltpu.CompilerParams(vmem_limit_bytes=32 << 20),
    )(gram, st, cor)


def on_device(state, range_test, corange_test):
    total_cells = state.shape[1] * NC
    st, gram, corange = gather(state, range_test, corange_test)
    return factor(gram, st, corange, float(total_cells) ** 0.5)


def solution(mesh):
    return jax.shard_map(
        on_device,
        mesh=mesh,
        in_specs=(P("tm", "cell"), P("tm", None), P(None, "cell")),
        out_specs=(P(("cell", "tm"), None), P(None, "tm")),
        check_vma=False,
    )
```

```python
import functools

import jax
import jax.numpy as jnp
from jax import lax
from jax.experimental import pallas as pl
from jax.experimental.pallas import tpu as pltpu
from jax.sharding import PartitionSpec as P

MESH = pl.DeviceIdType.MESH
F32, BF16 = jnp.float32, jnp.bfloat16
NY, NZ, NC = 4, 8, 8
RANK, STEPS, OWN, HALF = 128, 256, 512, 256
A = 80
SCALE = 32768.0
ORDER = (4, 3, 5, 2, 6, 1, 7, 0)
FAR_C = (4, 5, 3, 2, 6, 7, 1)

GROUPS = ((0, 1), (1, 2), (3, 2), (5, 2), (7, 1))
PLUS, MINUS = 0, 1
SCHEDULE = (
    ("g", 0), ("s", 0), ("g", 1), ("g", 2), ("s", 1), ("c", 0), ("g", 3), ("a", 0), ("b3", 0), ("g", 4),
    ("c", 1), ("g", 5), ("s", 2), ("b2", 1), ("g", 6), ("a", 1), ("g", 7), ("b2", 0), ("c", 2), ("y", 0),
    ("c", 3), ("b1", 1), ("s", 3), ("c", 4), ("c", 5), ("c", 6), ("a", 2), ("y", 1), ("A3",), ("c", 7),
    ("cs",), ("b1", 0), ("s", 4), ("a", 3), ("y", 2), ("A2",), ("b0",), ("r",), ("cq",), ("a", 4), ("y", 3),
    ("A1",), ("q",), ("y", 4),
)


def encode(x):
    s = x * x
    return (s * x * jnp.abs(x)).astype(BF16)


def decode(y):
    y = y.astype(F32)
    r = lax.rsqrt(lax.rsqrt(jnp.maximum(jnp.abs(y), 1.2e-38)))
    return jnp.where(y < 0, -r, r)


def span(h):
    return pl.ds(h * HALF, HALF)


def gather_kernel(state_hbm, r_hbm, c_hbm, st_out, gram_out, cor_out,
                  rbuf, rt, sfirst, sbuf, cbuf, part, cor,
                  sraw, rraw, sacc, racc, sz, rz, sb, rb, sraw2, rraw2, sacc2, racc2, crecv, cfull,
                  gpart, g1, g2, g3, g4,
                  load_sem, sem_raw, sem_acc, sem_z, sem_b, sem_raw2, sem_acc2,
                  sc, rc, sg1, rg1, sg2, rg2, sg3, rg3, sg4, rg4, out_sem):
    c, t = lax.axis_index("cell"), lax.axis_index("tm")
    y, z = t // NZ, lax.rem(t, NZ)

    def at_y(o):
        return (c, lax.rem(y + o, NY) * NZ + z)

    def at_z(o):
        return (c, y * NZ + lax.rem(z + o, NZ))

    def at_c(o):
        return (lax.rem(c + o, NC), t)

    barrier = pltpu.get_barrier_semaphore()
    peers = [at_y(1), at_y(NY - 1), at_z(1), at_z(NZ - 1)] + [at_c(o) for o in range(1, NC)]
    for p in peers:
        pl.semaphore_signal(barrier, inc=1, device_id=p, device_id_type=MESH)

    def load(hbm, buf, i, yo):
        cols = pl.ds(pl.multiple_of(lax.rem(y + yo, NY) * (NZ * OWN), NZ * OWN), NZ * OWN)
        return pltpu.make_async_copy(hbm.at[:, cols], buf.at[yo], load_sem.at[i, yo])

    load_r = pltpu.make_async_copy(r_hbm, rbuf, out_sem.at[3])
    load_r.start()

    def load_first(yo):
        chunk = lax.rem(y + yo, NY) * NZ + lax.rem(z + ORDER[0], NZ)
        cols = pl.ds(pl.multiple_of(chunk * OWN, OWN), OWN)
        return pltpu.make_async_copy(state_hbm.at[:, cols], sfirst.at[yo], load_sem.at[2, yo])

    for yo in range(NY):
        load_first(yo).start()
    for yo in range(NY):
        load(state_hbm, sbuf, 0, yo).start()
    for yo in range(NY):
        load(c_hbm, cbuf, 1, yo).start()

    load_r.wait()
    rt[...] = (rbuf[...].astype(F32) * SCALE).T.astype(BF16)

    to_y = (at_y(1), at_y(NY - 1))
    to_z = (at_z(1), at_z(NZ - 1))
    pending = []

    def message(src, dst, sems, i, to):
        return pltpu.make_async_remote_copy(
            src, dst, sems.at[(0,) + i], sems.at[(1,) + i], device_id=to, device_id_type=MESH)

    def send(copy):
        copy.start()
        pending.append(copy)

    def lanes(zo):
        return pl.ds(pl.multiple_of(lax.rem(z + zo, NZ) * OWN, OWN), OWN)

    def multiply(p):
        zo = ORDER[p]

        @pl.loop(0, NY)
        def _(yo):
            block = sfirst[yo] if p == 0 else sbuf[yo, :, lanes(zo)]
            part[zo, yo] = jnp.dot(rt[...], block, preferred_element_type=F32)

    def pa(zo, yo, h):
        return part[zo, yo, 0:A, span(h)]

    def pb(zo, yo, h):
        return part[zo, yo, A:RANK, span(h)]

    def raw_y(d, put, own):
        put(0, encode(own(2, d)))
        put(1, encode(own(1 if d == PLUS else 3, 1 - d)))

    def a_raw(g, d):
        at = pl.ds(*GROUPS[g])
        return message(sraw.at[d, at], rraw.at[d, at], sem_raw, (d, g), to_y[d])

    def a_acc(g, d):
        at = pl.ds(*GROUPS[g])
        return message(sacc.at[d, at], racc.at[d, at], sem_acc, (d, g), to_y[d])

    def positions(g):
        return range(GROUPS[g][0], GROUPS[g][0] + GROUPS[g][1])

    def sends(g):
        for d in (PLUS, MINUS):
            for p in positions(g):
                def put(slot, value):
                    sraw[d, p, slot] = value

                raw_y(d, put, lambda yo, h: pa(ORDER[p], yo, h))
            send(a_raw(g, d))

    def acc(g):
        for d in (PLUS, MINUS):
            a_raw(g, d).wait_recv()
            for p in positions(g):
                own = pa(ORDER[p], 1 if d == PLUS else 3, d)
                sacc[d, p] = encode(own + decode(rraw[d, p, 0]))
            send(a_acc(g, d))

    def z_msg(d, k, chain=0):
        i = (d, 4 - k)
        if k in (2, 3):
            return message(sz.at[i], rz.at[i], sem_z, i + (0,), to_z[d])
        return message(sz.at[i + (chain,)], rz.at[i + (chain,)], sem_z, i + (chain,), to_z[d])

    def toward(d, k):
        return k if d == PLUS else NZ - k

    def z_far():
        for d in (PLUS, MINUS):
            sz[d, 0, 0] = encode(pa(4, 0, d))
            send(z_msg(d, 4))

    def z_step(k):
        for d in (PLUS, MINUS):
            z_msg(d, k + 1).wait_recv()
            for chain in (0, 1):
                own = pa(toward(d, k), 0, d if chain == 0 else 1 - d)
                if k < 3 or chain == 0:
                    own = own + decode(rz[d, 3 - k, chain])
                sz[d, 4 - k, chain] = encode(own)
                if k == 1:
                    send(z_msg(d, k, chain))
            if k > 1:
                send(z_msg(d, k))

    def y_done(g):
        for d in (PLUS, MINUS):
            a_acc(g, d).wait_recv()
        for p in positions(g):
            zo = ORDER[p]
            for h in (0, 1):
                part[zo, 0, 0:A, span(h)] = pa(zo, 0, h) + decode(rraw[1 - h, p, 1]) + decode(racc[h, p])
        if g == 0:
            z_far()

    def b_msg(d, k, chain):
        i = (d, 4 - k, chain)
        return message(sb.at[i], rb.at[i], sem_b, i, to_z[d])

    def b_raw(d, k, chain):
        for yo in range(NY):
            sb[d, 4 - k, chain, yo] = encode(pb(toward(d, k), yo, d if chain == 0 else 1 - d))
        send(b_msg(d, k, chain))

    def b_step(k):
        def go(chain):
            for d in (PLUS, MINUS):
                b_msg(d, k + 1, chain).wait_recv()
                for yo in range(NY):
                    own = pb(toward(d, k), yo, d if chain == 0 else 1 - d)
                    sb[d, 4 - k, chain, yo] = encode(own + decode(rb[d, 3 - k, chain, yo]))
                send(b_msg(d, k, chain))

        return go

    def b_done():
        for d in (PLUS, MINUS):
            for chain in (0, 1):
                b_msg(d, 1, chain).wait_recv()
        for yo in range(NY):
            for h in (0, 1):
                part[0, yo, A:RANK, span(h)] = (
                    pb(0, yo, h) + decode(rb[h, 3, 0, yo]) + decode(rb[1 - h, 3, 1, yo]))

    def r_msg(d):
        return message(sraw2.at[d], rraw2.at[d], sem_raw2, (d,), to_y[d])

    def q_msg(d):
        return message(sacc2.at[d], racc2.at[d], sem_acc2, (d,), to_y[d])

    def raw2():
        for d in (PLUS, MINUS):
            def put(slot, value):
                sraw2[d, slot] = value

            raw_y(d, put, lambda yo, h: pb(0, yo, h))
            send(r_msg(d))

    def acc2():
        for d in (PLUS, MINUS):
            r_msg(d).wait_recv()
            sacc2[d] = encode(pb(0, 1 if d == PLUS else 3, d) + decode(rraw2[d, 0]))
            send(q_msg(d))

    def group(p):
        if p < 2:
            for yo in range(NY):
                (load(state_hbm, sbuf, 0, yo) if p else load_first(yo)).wait()
        multiply(p)
        if p == 0:
            pl.semaphore_wait(barrier, len(peers))
            b_raw(PLUS, 4, 0)
            b_raw(MINUS, 4, 0)
        if p in (1, 2):
            b_raw(p - 1, 3, 1)

    wide = NZ * OWN // 2

    def correlate(i):
        if i == 0:
            for yo in range(NY):
                load(c_hbm, cbuf, 1, yo).wait()
        cols = pl.ds(i % 2 * wide, wide)
        product = lax.dot_general(
            cbuf[i // 2, :, cols], sbuf[i // 2, :, cols], (((1,), (1,)), ((), ())), preferred_element_type=F32)
        cor[...] = product if i == 0 else cor[...] + product

    rows = 256 // NC

    def strip(i, n):
        return pl.ds(pl.multiple_of(i * n, n), n)

    def near_c(o):
        return lax.rem(c + o, NC)

    def cor_rs(o):
        return pltpu.make_async_remote_copy(
            cor.at[strip(near_c(o), rows)], crecv.at[o - 1], sc.at[0, o - 1], rc.at[0, o - 1],
            device_id=at_c(o), device_id_type=MESH)

    def cor_ag(o, owner):
        return pltpu.make_async_remote_copy(
            cfull.at[strip(owner, rows)], cfull.at[strip(owner, rows)], sc.at[1, o - 1], rc.at[1, owner],
            device_id=at_c(o), device_id_type=MESH)

    def cor_send():
        for o in FAR_C:
            cor_rs(o).start()

    def cor_sum():
        total = cor[strip(c, rows)]
        for o in range(1, NC):
            cor_rs(o).wait_recv()
            total = total + crecv[o - 1]
        cfull[strip(c, rows)] = total
        for o in FAR_C:
            cor_ag(o, c).start()

    acts = {
        "g": group, "s": sends, "a": acc, "y": y_done, "c": correlate, "cs": cor_send, "cq": cor_sum,
        "b3": b_step(3), "b2": b_step(2), "b1": b_step(1), "b0": b_done,
        "A3": lambda: z_step(3), "A2": lambda: z_step(2), "A1": lambda: z_step(1), "r": raw2, "q": acc2,
    }
    for act, *which in SCHEDULE:
        acts[act](*which)

    for d in (PLUS, MINUS):
        q_msg(d).wait_recv()
    for h in (0, 1):
        st_out[A:RANK, span(h)] = pb(0, 0, h) + decode(rraw2[1 - h, 1]) + decode(racc2[h])
    for d in (PLUS, MINUS):
        for chain in (0, 1):
            z_msg(d, 1, chain).wait_recv()
    for h in (0, 1):
        st_out[0:A, span(h)] = pa(0, 0, h) + decode(rz[h, 3, 0]) + decode(rz[1 - h, 3, 1])

    sk = st_out[...]
    gpart[...] = lax.dot_general(sk, sk, (((1,), (1,)), ((), ())),
                                 precision=lax.Precision.HIGHEST, preferred_element_type=F32)
    gr = RANK // NC

    def rs1(o):
        return pltpu.make_async_remote_copy(
            gpart.at[strip(near_c(o), gr)], g1.at[o - 1], sg1.at[o - 1], rg1.at[o - 1],
            device_id=at_c(o), device_id_type=MESH)

    def ag2(o, owner):
        return pltpu.make_async_remote_copy(
            g2.at[owner], g2.at[owner], sg2.at[o - 1], rg2.at[owner], device_id=at_y(o), device_id_type=MESH)

    def ag3(o, owner):
        return pltpu.make_async_remote_copy(
            g3.at[owner], g3.at[owner], sg3.at[o - 1], rg3.at[owner], device_id=at_z(o), device_id_type=MESH)

    def ag4(o, owner):
        return pltpu.make_async_remote_copy(
            g4.at[strip(owner, gr)], g4.at[strip(owner, gr)], sg4.at[o - 1], rg4.at[owner],
            device_id=at_c(o), device_id_type=MESH)

    for o in FAR_C:
        rs1(o).start()
    total = gpart[strip(c, gr)]
    for o in FAR_C[::-1]:
        rs1(o).wait_recv()
        total = total + g1[o - 1]
    g2[y] = total
    for o in (2, 1, 3):
        ag2(o, y).start()
    for o in range(1, NC):
        cor_ag(o, near_c(o)).wait_recv()
    cor_out[...] = cfull[...]
    for o in (1, 3, 2):
        ag2(o, lax.rem(y + o, NY)).wait_recv()
    total = g2[0]
    for i in range(1, NY):
        total = total + g2[i]
    g3[z] = total
    for o in (4, 3, 5, 2, 6, 1, 7):
        ag3(o, z).start()
    for copy in pending:
        copy.wait_send()
    for o in range(1, NC):
        cor_rs(o).wait_send()
        cor_ag(o, c).wait_send()
        rs1(o).wait_send()
    for o in range(1, NY):
        ag2(o, y).wait_send()
    for o in (1, 7, 2, 6, 3, 5, 4):
        ag3(o, lax.rem(z + o, NZ)).wait_recv()
    total = g3[0]
    for i in range(1, NZ):
        total = total + g3[i]
    g4[strip(c, gr)] = total
    for o in FAR_C:
        ag4(o, c).start()
    for o in range(1, NZ):
        ag3(o, z).wait_send()
    for o in FAR_C[::-1]:
        ag4(o, near_c(o)).wait_recv()
    gram_out[...] = g4[...]
    for o in range(1, NC):
        ag4(o, c).wait_send()


def gather(state, range_test, corange_test):
    dma = pltpu.SemaphoreType.DMA
    B = RANK - A

    def bf(*s):
        return pltpu.VMEM(s, BF16)

    def fl(*s):
        return pltpu.VMEM(s, F32)

    vmem = pl.BlockSpec(memory_space=pltpu.VMEM)
    hbm = pl.BlockSpec(memory_space=pl.ANY)
    return pl.pallas_call(
        gather_kernel,
        name="sketch_sums",
        out_shape=(pltpu.VMEM((RANK, OWN), F32), pltpu.VMEM((RANK, RANK), F32), pltpu.VMEM((256, 256), F32)),
        in_specs=[hbm, hbm, hbm],
        out_specs=(vmem, vmem, vmem),
        scratch_shapes=[
            bf(STEPS, RANK), bf(RANK, STEPS), bf(NY, STEPS, OWN), bf(NY, STEPS, NZ * OWN), bf(NY, 256, NZ * OWN), fl(NZ, NY, RANK, OWN), fl(256, 256),
            bf(2, NZ, 2, A, HALF), bf(2, NZ, 2, A, HALF), bf(2, NZ, A, HALF), bf(2, NZ, A, HALF),
            bf(2, 4, 2, A, HALF), bf(2, 4, 2, A, HALF), bf(2, 4, 2, NY, B, HALF), bf(2, 4, 2, NY, B, HALF),
            bf(2, 2, B, HALF), bf(2, 2, B, HALF), bf(2, B, HALF), bf(2, B, HALF),
            fl(7, 32, 256), fl(256, 256),
            fl(RANK, RANK), fl(7, 16, RANK), fl(NY, 16, RANK), fl(NZ, 16, RANK), fl(RANK, RANK),
            dma((3, NY)), dma((2, 2, 5)), dma((2, 2, 5)), dma((2, 2, 4, 2)), dma((2, 2, 4, 2)), dma((2, 2)), dma((2, 2)),
            dma((2, 7)), dma((2, NC)),
            dma((7,)), dma((7,)), dma((3,)), dma((NY,)), dma((7,)), dma((NZ,)), dma((7,)), dma((NC,)), dma((4,)),
        ],
        compiler_params=pltpu.CompilerParams(
            collective_id=1, has_side_effects=True, vmem_limit_bytes=60 << 20),
    )(state, range_test, corange_test)


def inverse_factor(w, scale):
    lane = lax.broadcasted_iota(jnp.int32, (8, RANK), 1)
    sub = lax.broadcasted_iota(jnp.int32, (8, RANK), 0)
    full = (8, RANK)
    out = []
    for b in range(RANK // 8):
        k = 8 * b
        inside = (lane >= k) & (lane < k + 8)
        cols = [jnp.broadcast_to(w[b][:, k + j:k + j + 1], full) for j in range(8)]
        p = [[jnp.broadcast_to(cols[j][i:i + 1], full) for j in range(i + 1)] for i in range(8)]
        l = [[None] * 8 for _ in range(8)]
        inv = []
        for j in range(8):
            inv.append(1.0 / p[j][j])
            for i in range(j + 1, 8):
                l[i][j] = p[i][j] * inv[j]
            for i in range(j + 1, 8):
                for m in range(j + 1, i + 1):
                    p[i][m] = p[i][m] - l[i][j] * p[m][j]
        own = jnp.where(inside, jnp.where(lane - k == sub, 1.0, 0.0), w[b])
        rows = []
        for i in range(8):
            r = jnp.broadcast_to(own[i:i + 1], full)
            for j in range(i):
                r = r - l[i][j] * rows[j]
            rows.append(r)
        done = jnp.zeros(full, F32)
        for i in range(8):
            done = jnp.where(sub == i, rows[i] * (scale * lax.rsqrt(p[i][i])), done)
        out.append(jnp.where(lane < k + 8, done, 0.0))
        for rb in range(b + 1, RANK // 8):
            q = []
            new = jnp.where(inside, 0.0, w[rb])
            for j in range(8):
                v = jnp.broadcast_to(w[rb][:, k + j:k + j + 1], full)
                for i in range(j):
                    v = v - q[i] * l[j][i]
                q.append(v)
            for j in range(8):
                new = new - (q[j] * inv[j]) * rows[j]
            w[rb] = new
    return jnp.concatenate(out, axis=0)


def factor_kernel(scale, gram, st, cor, out_hbm, cor_out, basis, w_ref, sem):
    store = pltpu.make_async_copy(cor, cor_out, sem.at[0])
    store.start()
    w = [gram[8 * b:8 * b + 8] for b in range(RANK // 8)]
    w_ref[...] = inverse_factor(w, scale)
    outs = []
    for h in (0, 1):
        basis[span(h)] = lax.dot_general(st[:, span(h)], w_ref[...], (((0,), (1,)), ((), ())),
                                         precision=lax.Precision.HIGHEST, preferred_element_type=F32)
        outs.append(pltpu.make_async_copy(basis.at[span(h)], out_hbm.at[span(h)], sem.at[1 + h]))
        outs[h].start()
    store.wait()
    for out in outs:
        out.wait()


def factor(gram, st, cor, scale):
    hbm = pl.BlockSpec(memory_space=pl.ANY)
    vmem = pl.BlockSpec(memory_space=pltpu.VMEM)
    return pl.pallas_call(
        functools.partial(factor_kernel, scale),
        name="factor",
        out_shape=(jax.ShapeDtypeStruct((OWN, RANK), F32), jax.ShapeDtypeStruct(cor.shape, F32)),
        in_specs=[vmem, vmem, vmem],
        out_specs=(hbm, hbm),
        scratch_shapes=[pltpu.VMEM((OWN, RANK), F32), pltpu.VMEM((RANK, RANK), F32), pltpu.SemaphoreType.DMA((3,))],
        compiler_params=pltpu.CompilerParams(vmem_limit_bytes=32 << 20),
    )(gram, st, cor)


def on_device(state, range_test, corange_test):
    total_cells = state.shape[1] * NC
    st, gram, corange = gather(state, range_test, corange_test)
    return factor(gram, st, corange, float(total_cells) ** 0.5)


def solution(mesh):
    return jax.shard_map(
        on_device,
        mesh=mesh,
        in_specs=(P("tm", "cell"), P("tm", None), P(None, "cell")),
        out_specs=(P(("cell", "tm"), None), P(None, "tm")),
        check_vma=False,
    )
```

```python
import functools

import jax
import jax.numpy as jnp
from jax import lax
from jax.experimental import pallas as pl
from jax.experimental.pallas import tpu as pltpu
from jax.sharding import PartitionSpec as P

MESH = pl.DeviceIdType.MESH
F32, BF16 = jnp.float32, jnp.bfloat16
NY, NZ, NC = 4, 8, 8
RANK, STEPS, OWN, HALF = 128, 256, 512, 256
A = 80
SCALE = 32768.0
ORDER = (4, 3, 5, 2, 6, 1, 7, 0)
FAR_C = (4, 5, 3, 2, 6, 7, 1)

GROUPS = ((0, 1), (1, 2), (3, 2), (5, 2), (7, 1))
PLUS, MINUS = 0, 1
SCHEDULE = (
    ("g", 0), ("s", 0), ("g", 1), ("g", 2), ("s", 1), ("g", 3), ("c", 0), ("g", 4), ("c", 1), ("b3", 0),
    ("a", 0), ("s", 2), ("g", 5), ("g", 6), ("c", 2), ("b2", 1), ("a", 1), ("c", 3), ("c", 4), ("y", 0),
    ("g", 7), ("b2", 0), ("c", 5), ("s", 3), ("c", 6), ("b1", 1), ("c", 7), ("cs",), ("y", 1), ("A3",),
    ("a", 2), ("b1", 0), ("s", 4), ("a", 3), ("y", 2), ("A2",), ("cq",), ("b0",), ("r",), ("a", 4), ("y", 3),
    ("A1",), ("q",), ("y", 4),
)


def encode(x):
    s = x * x
    return (s * x * jnp.abs(x)).astype(BF16)


def decode(y):
    y = y.astype(F32)
    r = lax.rsqrt(lax.rsqrt(jnp.maximum(jnp.abs(y), 1.2e-38)))
    return jnp.where(y < 0, -r, r)


def span(h):
    return pl.ds(h * HALF, HALF)


def gather_kernel(state_hbm, r_hbm, c_hbm, st_out, gram_out, cor_out,
                  rbuf, rt, sbuf, cbuf, part, cor,
                  sraw, rraw, sacc, racc, sz, rz, sb, rb, sraw2, rraw2, sacc2, racc2, crecv, cfull,
                  gpart, g1, g2, g3, g4,
                  load_sem, sem_raw, sem_acc, sem_z, sem_b, sem_raw2, sem_acc2,
                  sc, rc, sg1, rg1, sg2, rg2, sg3, rg3, sg4, rg4, out_sem):
    c, t = lax.axis_index("cell"), lax.axis_index("tm")
    y, z = t // NZ, lax.rem(t, NZ)

    def at_y(o):
        return (c, lax.rem(y + o, NY) * NZ + z)

    def at_z(o):
        return (c, y * NZ + lax.rem(z + o, NZ))

    def at_c(o):
        return (lax.rem(c + o, NC), t)

    barrier = pltpu.get_barrier_semaphore()
    peers = [at_y(o) for o in range(1, NY)] + [at_z(o) for o in range(1, NZ)] + [at_c(o) for o in range(1, NC)]
    for p in peers:
        pl.semaphore_signal(barrier, inc=1, device_id=p, device_id_type=MESH)

    def load(hbm, buf, i, yo):
        cols = pl.ds(pl.multiple_of(lax.rem(y + yo, NY) * (NZ * OWN), NZ * OWN), NZ * OWN)
        return pltpu.make_async_copy(hbm.at[:, cols], buf.at[yo], load_sem.at[i, yo])

    load_r = pltpu.make_async_copy(r_hbm, rbuf, out_sem.at[3])
    load_r.start()
    for yo in range(NY):
        load(state_hbm, sbuf, 0, yo).start()
    for yo in range(NY):
        load(c_hbm, cbuf, 1, yo).start()

    load_r.wait()
    rt[...] = (rbuf[...].astype(F32) * SCALE).T.astype(BF16)

    to_y = (at_y(1), at_y(NY - 1))
    to_z = (at_z(1), at_z(NZ - 1))
    pending = []

    def message(src, dst, sems, i, to):
        return pltpu.make_async_remote_copy(
            src, dst, sems.at[(0,) + i], sems.at[(1,) + i], device_id=to, device_id_type=MESH)

    def send(copy):
        copy.start()
        pending.append(copy)

    def lanes(zo):
        return pl.ds(pl.multiple_of(lax.rem(z + zo, NZ) * OWN, OWN), OWN)

    def multiply(p):
        zo = ORDER[p]

        @pl.loop(0, NY)
        def _(yo):
            part[zo, yo] = jnp.dot(rt[...], sbuf[yo, :, lanes(zo)], preferred_element_type=F32)

    def pa(zo, yo, h):
        return part[zo, yo, 0:A, span(h)]

    def pb(zo, yo, h):
        return part[zo, yo, A:RANK, span(h)]

    def raw_y(d, put, own):
        put(0, encode(own(2, d)))
        put(1, encode(own(1 if d == PLUS else 3, 1 - d)))

    def a_raw(g, d):
        at = pl.ds(*GROUPS[g])
        return message(sraw.at[d, at], rraw.at[d, at], sem_raw, (d, g), to_y[d])

    def a_acc(g, d):
        at = pl.ds(*GROUPS[g])
        return message(sacc.at[d, at], racc.at[d, at], sem_acc, (d, g), to_y[d])

    def positions(g):
        return range(GROUPS[g][0], GROUPS[g][0] + GROUPS[g][1])

    def sends(g):
        for d in (PLUS, MINUS):
            for p in positions(g):
                def put(slot, value):
                    sraw[d, p, slot] = value

                raw_y(d, put, lambda yo, h: pa(ORDER[p], yo, h))
            send(a_raw(g, d))

    def acc(g):
        for d in (PLUS, MINUS):
            a_raw(g, d).wait_recv()
            for p in positions(g):
                own = pa(ORDER[p], 1 if d == PLUS else 3, d)
                sacc[d, p] = encode(own + decode(rraw[d, p, 0]))
            send(a_acc(g, d))

    def z_msg(d, k):
        src, dst = (sz.at[d, 0, 0], rz.at[d, 0, 0]) if k == 4 else (sz.at[d, 4 - k], rz.at[d, 4 - k])
        return message(src, dst, sem_z, (d, 4 - k), to_z[d])

    def toward(d, k):
        return k if d == PLUS else NZ - k

    def z_far():
        for d in (PLUS, MINUS):
            sz[d, 0, 0] = encode(pa(4, 0, d))
            send(z_msg(d, 4))

    def z_step(k):
        for d in (PLUS, MINUS):
            zo = toward(d, k)
            z_msg(d, k + 1).wait_recv()
            sz[d, 4 - k, 0] = encode(pa(zo, 0, d) + decode(rz[d, 3 - k, 0]))
            other = pa(zo, 0, 1 - d)
            sz[d, 4 - k, 1] = encode(other if k == 3 else other + decode(rz[d, 3 - k, 1]))
            send(z_msg(d, k))

    def y_done(g):
        for d in (PLUS, MINUS):
            a_acc(g, d).wait_recv()
        for p in positions(g):
            zo = ORDER[p]
            for h in (0, 1):
                part[zo, 0, 0:A, span(h)] = pa(zo, 0, h) + decode(rraw[1 - h, p, 1]) + decode(racc[h, p])
        if g == 0:
            z_far()

    def b_msg(d, k, chain):
        i = (d, 4 - k, chain)
        return message(sb.at[i], rb.at[i], sem_b, i, to_z[d])

    def b_raw(d, k, chain):
        for yo in range(NY):
            sb[d, 4 - k, chain, yo] = encode(pb(toward(d, k), yo, d if chain == 0 else 1 - d))
        send(b_msg(d, k, chain))

    def b_step(k):
        def go(chain):
            for d in (PLUS, MINUS):
                b_msg(d, k + 1, chain).wait_recv()
                for yo in range(NY):
                    own = pb(toward(d, k), yo, d if chain == 0 else 1 - d)
                    sb[d, 4 - k, chain, yo] = encode(own + decode(rb[d, 3 - k, chain, yo]))
                send(b_msg(d, k, chain))

        return go

    def b_done():
        for d in (PLUS, MINUS):
            for chain in (0, 1):
                b_msg(d, 1, chain).wait_recv()
        for yo in range(NY):
            for h in (0, 1):
                part[0, yo, A:RANK, span(h)] = (
                    pb(0, yo, h) + decode(rb[h, 3, 0, yo]) + decode(rb[1 - h, 3, 1, yo]))

    def r_msg(d):
        return message(sraw2.at[d], rraw2.at[d], sem_raw2, (d,), to_y[d])

    def q_msg(d):
        return message(sacc2.at[d], racc2.at[d], sem_acc2, (d,), to_y[d])

    def raw2():
        for d in (PLUS, MINUS):
            def put(slot, value):
                sraw2[d, slot] = value

            raw_y(d, put, lambda yo, h: pb(0, yo, h))
            send(r_msg(d))

    def acc2():
        for d in (PLUS, MINUS):
            r_msg(d).wait_recv()
            sacc2[d] = encode(pb(0, 1 if d == PLUS else 3, d) + decode(rraw2[d, 0]))
            send(q_msg(d))

    def group(p):
        if p == 0:
            for yo in range(NY):
                load(state_hbm, sbuf, 0, yo).wait()
        multiply(p)
        if p == 0:
            pl.semaphore_wait(barrier, len(peers))
            b_raw(PLUS, 4, 0)
            b_raw(MINUS, 4, 0)
        if p in (1, 2):
            b_raw(p - 1, 3, 1)

    wide = NZ * OWN // 2

    def correlate(i):
        if i == 0:
            for yo in range(NY):
                load(c_hbm, cbuf, 1, yo).wait()
        cols = pl.ds(i % 2 * wide, wide)
        product = lax.dot_general(
            cbuf[i // 2, :, cols], sbuf[i // 2, :, cols], (((1,), (1,)), ((), ())), preferred_element_type=F32)
        cor[...] = product if i == 0 else cor[...] + product

    rows = 256 // NC

    def strip(i, n):
        return pl.ds(pl.multiple_of(i * n, n), n)

    def near_c(o):
        return lax.rem(c + o, NC)

    def cor_rs(o):
        return pltpu.make_async_remote_copy(
            cor.at[strip(near_c(o), rows)], crecv.at[o - 1], sc.at[0, o - 1], rc.at[0, o - 1],
            device_id=at_c(o), device_id_type=MESH)

    def cor_ag(o, owner):
        return pltpu.make_async_remote_copy(
            cfull.at[strip(owner, rows)], cfull.at[strip(owner, rows)], sc.at[1, o - 1], rc.at[1, owner],
            device_id=at_c(o), device_id_type=MESH)

    def cor_send():
        for o in FAR_C:
            cor_rs(o).start()

    def cor_sum():
        total = cor[strip(c, rows)]
        for o in range(1, NC):
            cor_rs(o).wait_recv()
            total = total + crecv[o - 1]
        cfull[strip(c, rows)] = total
        for o in FAR_C:
            cor_ag(o, c).start()

    acts = {
        "g": group, "s": sends, "a": acc, "y": y_done, "c": correlate, "cs": cor_send, "cq": cor_sum,
        "b3": b_step(3), "b2": b_step(2), "b1": b_step(1), "b0": b_done,
        "A3": lambda: z_step(3), "A2": lambda: z_step(2), "A1": lambda: z_step(1), "r": raw2, "q": acc2,
    }
    for act, *which in SCHEDULE:
        acts[act](*which)

    for d in (PLUS, MINUS):
        q_msg(d).wait_recv()
    for h in (0, 1):
        st_out[A:RANK, span(h)] = pb(0, 0, h) + decode(rraw2[1 - h, 1]) + decode(racc2[h])
    for d in (PLUS, MINUS):
        z_msg(d, 1).wait_recv()
    for h in (0, 1):
        st_out[0:A, span(h)] = pa(0, 0, h) + decode(rz[h, 3, 0]) + decode(rz[1 - h, 3, 1])

    sk = st_out[...]
    gpart[...] = lax.dot_general(sk, sk, (((1,), (1,)), ((), ())),
                                 precision=lax.Precision.HIGHEST, preferred_element_type=F32)
    gr = RANK // NC

    def rs1(o):
        return pltpu.make_async_remote_copy(
            gpart.at[strip(near_c(o), gr)], g1.at[o - 1], sg1.at[o - 1], rg1.at[o - 1],
            device_id=at_c(o), device_id_type=MESH)

    def ag2(o, owner):
        return pltpu.make_async_remote_copy(
            g2.at[owner], g2.at[owner], sg2.at[o - 1], rg2.at[owner], device_id=at_y(o), device_id_type=MESH)

    def ag3(o, owner):
        return pltpu.make_async_remote_copy(
            g3.at[owner], g3.at[owner], sg3.at[o - 1], rg3.at[owner], device_id=at_z(o), device_id_type=MESH)

    def ag4(o, owner):
        return pltpu.make_async_remote_copy(
            g4.at[strip(owner, gr)], g4.at[strip(owner, gr)], sg4.at[o - 1], rg4.at[owner],
            device_id=at_c(o), device_id_type=MESH)

    for o in FAR_C:
        rs1(o).start()
    total = gpart[strip(c, gr)]
    for o in FAR_C[::-1]:
        rs1(o).wait_recv()
        total = total + g1[o - 1]
    g2[y] = total
    for o in (2, 1, 3):
        ag2(o, y).start()
    for o in range(1, NC):
        cor_ag(o, near_c(o)).wait_recv()
    cor_out[...] = cfull[...]
    for o in (1, 3, 2):
        ag2(o, lax.rem(y + o, NY)).wait_recv()
    total = g2[0]
    for i in range(1, NY):
        total = total + g2[i]
    g3[z] = total
    for o in (4, 3, 5, 2, 6, 1, 7):
        ag3(o, z).start()
    for copy in pending:
        copy.wait_send()
    for o in range(1, NC):
        cor_rs(o).wait_send()
        cor_ag(o, c).wait_send()
        rs1(o).wait_send()
    for o in range(1, NY):
        ag2(o, y).wait_send()
    for o in (1, 7, 2, 6, 3, 5, 4):
        ag3(o, lax.rem(z + o, NZ)).wait_recv()
    total = g3[0]
    for i in range(1, NZ):
        total = total + g3[i]
    g4[strip(c, gr)] = total
    for o in FAR_C:
        ag4(o, c).start()
    for o in range(1, NZ):
        ag3(o, z).wait_send()
    for o in FAR_C[::-1]:
        ag4(o, near_c(o)).wait_recv()
    gram_out[...] = g4[...]
    for o in range(1, NC):
        ag4(o, c).wait_send()


def gather(state, range_test, corange_test):
    dma = pltpu.SemaphoreType.DMA
    B = RANK - A

    def bf(*s):
        return pltpu.VMEM(s, BF16)

    def fl(*s):
        return pltpu.VMEM(s, F32)

    vmem = pl.BlockSpec(memory_space=pltpu.VMEM)
    hbm = pl.BlockSpec(memory_space=pl.ANY)
    return pl.pallas_call(
        gather_kernel,
        name="sketch_sums",
        out_shape=(pltpu.VMEM((RANK, OWN), F32), pltpu.VMEM((RANK, RANK), F32), pltpu.VMEM((256, 256), F32)),
        in_specs=[hbm, hbm, hbm],
        out_specs=(vmem, vmem, vmem),
        scratch_shapes=[
            bf(STEPS, RANK), bf(RANK, STEPS), bf(NY, STEPS, NZ * OWN), bf(NY, 256, NZ * OWN), fl(NZ, NY, RANK, OWN), fl(256, 256),
            bf(2, NZ, 2, A, HALF), bf(2, NZ, 2, A, HALF), bf(2, NZ, A, HALF), bf(2, NZ, A, HALF),
            bf(2, 4, 2, A, HALF), bf(2, 4, 2, A, HALF), bf(2, 4, 2, NY, B, HALF), bf(2, 4, 2, NY, B, HALF),
            bf(2, 2, B, HALF), bf(2, 2, B, HALF), bf(2, B, HALF), bf(2, B, HALF),
            fl(7, 32, 256), fl(256, 256),
            fl(RANK, RANK), fl(7, 16, RANK), fl(NY, 16, RANK), fl(NZ, 16, RANK), fl(RANK, RANK),
            dma((2, NY)), dma((2, 2, 5)), dma((2, 2, 5)), dma((2, 2, 4)), dma((2, 2, 4, 2)), dma((2, 2)), dma((2, 2)),
            dma((2, 7)), dma((2, NC)),
            dma((7,)), dma((7,)), dma((3,)), dma((NY,)), dma((7,)), dma((NZ,)), dma((7,)), dma((NC,)), dma((4,)),
        ],
        compiler_params=pltpu.CompilerParams(
            collective_id=1, has_side_effects=True, vmem_limit_bytes=60 << 20),
    )(state, range_test, corange_test)


def inverse_factor(w, scale):
    lane = lax.broadcasted_iota(jnp.int32, (8, RANK), 1)
    sub = lax.broadcasted_iota(jnp.int32, (8, RANK), 0)
    full = (8, RANK)
    out = []
    for b in range(RANK // 8):
        k = 8 * b
        inside = (lane >= k) & (lane < k + 8)
        cols = [jnp.broadcast_to(w[b][:, k + j:k + j + 1], full) for j in range(8)]
        p = [[jnp.broadcast_to(cols[j][i:i + 1], full) for j in range(i + 1)] for i in range(8)]
        l = [[None] * 8 for _ in range(8)]
        inv = []
        for j in range(8):
            inv.append(1.0 / p[j][j])
            for i in range(j + 1, 8):
                l[i][j] = p[i][j] * inv[j]
            for i in range(j + 1, 8):
                for m in range(j + 1, i + 1):
                    p[i][m] = p[i][m] - l[i][j] * p[m][j]
        own = jnp.where(inside, jnp.where(lane - k == sub, 1.0, 0.0), w[b])
        rows = []
        for i in range(8):
            r = jnp.broadcast_to(own[i:i + 1], full)
            for j in range(i):
                r = r - l[i][j] * rows[j]
            rows.append(r)
        done = jnp.zeros(full, F32)
        for i in range(8):
            done = jnp.where(sub == i, rows[i] * (scale * lax.rsqrt(p[i][i])), done)
        out.append(jnp.where(lane < k + 8, done, 0.0))
        for rb in range(b + 1, RANK // 8):
            q = []
            new = jnp.where(inside, 0.0, w[rb])
            for j in range(8):
                v = jnp.broadcast_to(w[rb][:, k + j:k + j + 1], full)
                for i in range(j):
                    v = v - q[i] * l[j][i]
                q.append(v)
            t = [(q[j] * inv[j]) * rows[j] for j in range(8)]
            w[rb] = new - (((t[0] + t[1]) + (t[2] + t[3])) + ((t[4] + t[5]) + (t[6] + t[7])))
    return jnp.concatenate(out, axis=0)


def factor_kernel(scale, gram, st, cor, out_hbm, cor_out, basis, w_ref, sem):
    store = pltpu.make_async_copy(cor, cor_out, sem.at[0])
    store.start()
    w = [gram[8 * b:8 * b + 8] for b in range(RANK // 8)]
    w_ref[...] = inverse_factor(w, scale)
    basis[...] = lax.dot_general(st[...], w_ref[...], (((0,), (1,)), ((), ())),
                                 precision=lax.Precision.HIGHEST, preferred_element_type=F32)
    out = pltpu.make_async_copy(basis, out_hbm, sem.at[1])
    out.start()
    store.wait()
    out.wait()


def factor(gram, st, cor, scale):
    hbm = pl.BlockSpec(memory_space=pl.ANY)
    vmem = pl.BlockSpec(memory_space=pltpu.VMEM)
    return pl.pallas_call(
        functools.partial(factor_kernel, scale),
        name="factor",
        out_shape=(jax.ShapeDtypeStruct((OWN, RANK), F32), jax.ShapeDtypeStruct(cor.shape, F32)),
        in_specs=[vmem, vmem, vmem],
        out_specs=(hbm, hbm),
        scratch_shapes=[pltpu.VMEM((OWN, RANK), F32), pltpu.VMEM((RANK, RANK), F32), pltpu.SemaphoreType.DMA((2,))],
        compiler_params=pltpu.CompilerParams(vmem_limit_bytes=32 << 20),
    )(gram, st, cor)


def on_device(state, range_test, corange_test):
    total_cells = state.shape[1] * NC
    st, gram, corange = gather(state, range_test, corange_test)
    return factor(gram, st, corange, float(total_cells) ** 0.5)


def solution(mesh):
    return jax.shard_map(
        on_device,
        mesh=mesh,
        in_specs=(P("tm", "cell"), P("tm", None), P(None, "cell")),
        out_specs=(P(("cell", "tm"), None), P(None, "tm")),
        check_vma=False,
    )
```

```python
import functools

import jax
import jax.numpy as jnp
from jax import lax
from jax.experimental import pallas as pl
from jax.experimental.pallas import tpu as pltpu
from jax.sharding import PartitionSpec as P

MESH = pl.DeviceIdType.MESH
F32, BF16 = jnp.float32, jnp.bfloat16
NY, NZ, NC = 4, 8, 8
RANK, STEPS, OWN, HALF = 128, 256, 512, 256
A = 80
SCALE = 32768.0
ORDER = (4, 3, 5, 2, 6, 1, 7, 0)
FAR_C = (4, 5, 3, 2, 6, 7, 1)

GROUPS = ((0, 1), (1, 2), (3, 2), (5, 2), (7, 1))
PLUS, MINUS = 0, 1
SCHEDULE = (
    ("g", 0), ("s", 0), ("g", 1), ("g", 2), ("s", 1), ("g", 3), ("c", 0), ("g", 4), ("c", 1), ("b3", 0),
    ("a", 0), ("s", 2), ("g", 5), ("g", 6), ("c", 2), ("b2", 1), ("a", 1), ("c", 3), ("c", 4), ("y", 0),
    ("g", 7), ("b2", 0), ("c", 5), ("s", 3), ("c", 6), ("b1", 1), ("c", 7), ("cs",), ("y", 1), ("A3",),
    ("a", 2), ("b1", 0), ("s", 4), ("a", 3), ("y", 2), ("A2",), ("cq",), ("b0",), ("r",), ("a", 4), ("y", 3),
    ("A1",), ("q",), ("y", 4),
)


def encode(x):
    s = x * x
    return (s * x * jnp.abs(x)).astype(BF16)


def decode(y):
    y = y.astype(F32)
    r = lax.rsqrt(lax.rsqrt(jnp.maximum(jnp.abs(y), 1.2e-38)))
    return jnp.where(y < 0, -r, r)


def span(h):
    return pl.ds(h * HALF, HALF)


def gather_kernel(state_hbm, r_hbm, c_hbm, st_out, gram_out, cor_out,
                  rbuf, rt, sbuf, cbuf, part, cor,
                  sraw, rraw, sacc, racc, sz, rz, sb, rb, sraw2, rraw2, sacc2, racc2, crecv, cfull,
                  gpart, g1, g2, g3, g4,
                  load_sem, sem_raw, sem_acc, sem_z, sem_b, sem_raw2, sem_acc2,
                  sc, rc, sg1, rg1, sg2, rg2, sg3, rg3, sg4, rg4, out_sem):
    c, t = lax.axis_index("cell"), lax.axis_index("tm")
    y, z = t // NZ, lax.rem(t, NZ)

    def at_y(o):
        return (c, lax.rem(y + o, NY) * NZ + z)

    def at_z(o):
        return (c, y * NZ + lax.rem(z + o, NZ))

    def at_c(o):
        return (lax.rem(c + o, NC), t)

    barrier = pltpu.get_barrier_semaphore()
    peers = [at_y(o) for o in range(1, NY)] + [at_z(o) for o in range(1, NZ)] + [at_c(o) for o in range(1, NC)]
    for p in peers:
        pl.semaphore_signal(barrier, inc=1, device_id=p, device_id_type=MESH)

    def load(hbm, buf, i, yo):
        cols = pl.ds(pl.multiple_of(lax.rem(y + yo, NY) * (NZ * OWN), NZ * OWN), NZ * OWN)
        return pltpu.make_async_copy(hbm.at[:, cols], buf.at[yo], load_sem.at[i, yo])

    load_r = pltpu.make_async_copy(r_hbm, rbuf, out_sem.at[3])
    load_r.start()
    for yo in range(NY):
        load(state_hbm, sbuf, 0, yo).start()
    for yo in range(NY):
        load(c_hbm, cbuf, 1, yo).start()

    load_r.wait()
    rt[...] = (rbuf[...].astype(F32) * SCALE).T.astype(BF16)

    to_y = (at_y(1), at_y(NY - 1))
    to_z = (at_z(1), at_z(NZ - 1))
    pending = []

    def message(src, dst, sems, i, to):
        return pltpu.make_async_remote_copy(
            src, dst, sems.at[(0,) + i], sems.at[(1,) + i], device_id=to, device_id_type=MESH)

    def send(copy):
        copy.start()
        pending.append(copy)

    def lanes(zo):
        return pl.ds(pl.multiple_of(lax.rem(z + zo, NZ) * OWN, OWN), OWN)

    def multiply(p):
        zo = ORDER[p]

        @pl.loop(0, NY)
        def _(yo):
            part[zo, yo] = jnp.dot(rt[...], sbuf[yo, :, lanes(zo)], preferred_element_type=F32)

    def pa(zo, yo, h):
        return part[zo, yo, 0:A, span(h)]

    def pb(zo, yo, h):
        return part[zo, yo, A:RANK, span(h)]

    def raw_y(d, put, own):
        put(0, encode(own(2, d)))
        put(1, encode(own(1 if d == PLUS else 3, 1 - d)))

    def a_raw(g, d):
        at = pl.ds(*GROUPS[g])
        return message(sraw.at[d, at], rraw.at[d, at], sem_raw, (d, g), to_y[d])

    def a_acc(g, d):
        at = pl.ds(*GROUPS[g])
        return message(sacc.at[d, at], racc.at[d, at], sem_acc, (d, g), to_y[d])

    def positions(g):
        return range(GROUPS[g][0], GROUPS[g][0] + GROUPS[g][1])

    def sends(g):
        for d in (PLUS, MINUS):
            for p in positions(g):
                def put(slot, value):
                    sraw[d, p, slot] = value

                raw_y(d, put, lambda yo, h: pa(ORDER[p], yo, h))
            send(a_raw(g, d))

    def acc(g):
        for d in (PLUS, MINUS):
            a_raw(g, d).wait_recv()
            for p in positions(g):
                own = pa(ORDER[p], 1 if d == PLUS else 3, d)
                sacc[d, p] = encode(own + decode(rraw[d, p, 0]))
            send(a_acc(g, d))

    def z_msg(d, k):
        src, dst = (sz.at[d, 0, 0], rz.at[d, 0, 0]) if k == 4 else (sz.at[d, 4 - k], rz.at[d, 4 - k])
        return message(src, dst, sem_z, (d, 4 - k), to_z[d])

    def toward(d, k):
        return k if d == PLUS else NZ - k

    def z_far():
        for d in (PLUS, MINUS):
            sz[d, 0, 0] = encode(pa(4, 0, d))
            send(z_msg(d, 4))

    def z_step(k):
        for d in (PLUS, MINUS):
            zo = toward(d, k)
            z_msg(d, k + 1).wait_recv()
            sz[d, 4 - k, 0] = encode(pa(zo, 0, d) + decode(rz[d, 3 - k, 0]))
            other = pa(zo, 0, 1 - d)
            sz[d, 4 - k, 1] = encode(other if k == 3 else other + decode(rz[d, 3 - k, 1]))
            send(z_msg(d, k))

    def y_done(g):
        for d in (PLUS, MINUS):
            a_acc(g, d).wait_recv()
        for p in positions(g):
            zo = ORDER[p]
            for h in (0, 1):
                part[zo, 0, 0:A, span(h)] = pa(zo, 0, h) + decode(rraw[1 - h, p, 1]) + decode(racc[h, p])
        if g == 0:
            z_far()

    def b_msg(d, k, chain):
        i = (d, 4 - k, chain)
        return message(sb.at[i], rb.at[i], sem_b, i, to_z[d])

    def b_raw(d, k, chain):
        for yo in range(NY):
            sb[d, 4 - k, chain, yo] = encode(pb(toward(d, k), yo, d if chain == 0 else 1 - d))
        send(b_msg(d, k, chain))

    def b_step(k):
        def go(chain):
            for d in (PLUS, MINUS):
                b_msg(d, k + 1, chain).wait_recv()
                for yo in range(NY):
                    own = pb(toward(d, k), yo, d if chain == 0 else 1 - d)
                    sb[d, 4 - k, chain, yo] = encode(own + decode(rb[d, 3 - k, chain, yo]))
                send(b_msg(d, k, chain))

        return go

    def b_done():
        for d in (PLUS, MINUS):
            for chain in (0, 1):
                b_msg(d, 1, chain).wait_recv()
        for yo in range(NY):
            for h in (0, 1):
                part[0, yo, A:RANK, span(h)] = (
                    pb(0, yo, h) + decode(rb[h, 3, 0, yo]) + decode(rb[1 - h, 3, 1, yo]))

    def r_msg(d):
        return message(sraw2.at[d], rraw2.at[d], sem_raw2, (d,), to_y[d])

    def q_msg(d):
        return message(sacc2.at[d], racc2.at[d], sem_acc2, (d,), to_y[d])

    def raw2():
        for d in (PLUS, MINUS):
            def put(slot, value):
                sraw2[d, slot] = value

            raw_y(d, put, lambda yo, h: pb(0, yo, h))
            send(r_msg(d))

    def acc2():
        for d in (PLUS, MINUS):
            r_msg(d).wait_recv()
            sacc2[d] = encode(pb(0, 1 if d == PLUS else 3, d) + decode(rraw2[d, 0]))
            send(q_msg(d))

    def group(p):
        if p == 0:
            for yo in range(NY):
                load(state_hbm, sbuf, 0, yo).wait()
        multiply(p)
        if p == 0:
            pl.semaphore_wait(barrier, len(peers))
            b_raw(PLUS, 4, 0)
            b_raw(MINUS, 4, 0)
        if p in (1, 2):
            b_raw(p - 1, 3, 1)

    wide = NZ * OWN // 2

    def correlate(i):
        if i == 0:
            for yo in range(NY):
                load(c_hbm, cbuf, 1, yo).wait()
        cols = pl.ds(i % 2 * wide, wide)
        product = lax.dot_general(
            cbuf[i // 2, :, cols], sbuf[i // 2, :, cols], (((1,), (1,)), ((), ())), preferred_element_type=F32)
        cor[...] = product if i == 0 else cor[...] + product

    rows = 256 // NC

    def strip(i, n):
        return pl.ds(pl.multiple_of(i * n, n), n)

    def near_c(o):
        return lax.rem(c + o, NC)

    def cor_rs(o):
        return pltpu.make_async_remote_copy(
            cor.at[strip(near_c(o), rows)], crecv.at[o - 1], sc.at[0, o - 1], rc.at[0, o - 1],
            device_id=at_c(o), device_id_type=MESH)

    def cor_ag(o, owner):
        return pltpu.make_async_remote_copy(
            cfull.at[strip(owner, rows)], cfull.at[strip(owner, rows)], sc.at[1, o - 1], rc.at[1, owner],
            device_id=at_c(o), device_id_type=MESH)

    def cor_send():
        for o in FAR_C:
            cor_rs(o).start()

    def cor_sum():
        total = cor[strip(c, rows)]
        for o in range(1, NC):
            cor_rs(o).wait_recv()
            total = total + crecv[o - 1]
        cfull[strip(c, rows)] = total
        for o in FAR_C:
            cor_ag(o, c).start()

    acts = {
        "g": group, "s": sends, "a": acc, "y": y_done, "c": correlate, "cs": cor_send, "cq": cor_sum,
        "b3": b_step(3), "b2": b_step(2), "b1": b_step(1), "b0": b_done,
        "A3": lambda: z_step(3), "A2": lambda: z_step(2), "A1": lambda: z_step(1), "r": raw2, "q": acc2,
    }
    for act, *which in SCHEDULE:
        acts[act](*which)

    for d in (PLUS, MINUS):
        q_msg(d).wait_recv()
    for h in (0, 1):
        st_out[A:RANK, span(h)] = pb(0, 0, h) + decode(rraw2[1 - h, 1]) + decode(racc2[h])
    for d in (PLUS, MINUS):
        z_msg(d, 1).wait_recv()
    for h in (0, 1):
        st_out[0:A, span(h)] = pa(0, 0, h) + decode(rz[h, 3, 0]) + decode(rz[1 - h, 3, 1])

    sk = st_out[...]
    gpart[...] = lax.dot_general(sk, sk, (((1,), (1,)), ((), ())),
                                 precision=lax.Precision.HIGHEST, preferred_element_type=F32)
    gr = RANK // NC

    def rs1(o):
        return pltpu.make_async_remote_copy(
            gpart.at[strip(near_c(o), gr)], g1.at[o - 1], sg1.at[o - 1], rg1.at[o - 1],
            device_id=at_c(o), device_id_type=MESH)

    def ag2(o, owner):
        return pltpu.make_async_remote_copy(
            g2.at[owner], g2.at[owner], sg2.at[o - 1], rg2.at[owner], device_id=at_y(o), device_id_type=MESH)

    def ag3(o, owner):
        return pltpu.make_async_remote_copy(
            g3.at[owner], g3.at[owner], sg3.at[o - 1], rg3.at[owner], device_id=at_z(o), device_id_type=MESH)

    def ag4(o, owner):
        return pltpu.make_async_remote_copy(
            g4.at[strip(owner, gr)], g4.at[strip(owner, gr)], sg4.at[o - 1], rg4.at[owner],
            device_id=at_c(o), device_id_type=MESH)

    for o in FAR_C:
        rs1(o).start()
    total = gpart[strip(c, gr)]
    for o in FAR_C[::-1]:
        rs1(o).wait_recv()
        total = total + g1[o - 1]
    g2[y] = total
    for o in (2, 1, 3):
        ag2(o, y).start()
    for o in range(1, NC):
        cor_ag(o, near_c(o)).wait_recv()
    cor_out[...] = cfull[...]
    for o in (1, 3, 2):
        ag2(o, lax.rem(y + o, NY)).wait_recv()
    total = g2[0]
    for i in range(1, NY):
        total = total + g2[i]
    g3[z] = total
    for o in (4, 3, 5, 2, 6, 1, 7):
        ag3(o, z).start()
    for copy in pending:
        copy.wait_send()
    for o in range(1, NC):
        cor_rs(o).wait_send()
        cor_ag(o, c).wait_send()
        rs1(o).wait_send()
    for o in range(1, NY):
        ag2(o, y).wait_send()
    for o in (1, 7, 2, 6, 3, 5, 4):
        ag3(o, lax.rem(z + o, NZ)).wait_recv()
    total = g3[0]
    for i in range(1, NZ):
        total = total + g3[i]
    g4[strip(c, gr)] = total
    for o in FAR_C:
        ag4(o, c).start()
    for o in range(1, NZ):
        ag3(o, z).wait_send()
    for o in FAR_C[::-1]:
        ag4(o, near_c(o)).wait_recv()
    gram_out[...] = g4[...]
    for o in range(1, NC):
        ag4(o, c).wait_send()


def gather(state, range_test, corange_test):
    dma = pltpu.SemaphoreType.DMA
    B = RANK - A

    def bf(*s):
        return pltpu.VMEM(s, BF16)

    def fl(*s):
        return pltpu.VMEM(s, F32)

    vmem = pl.BlockSpec(memory_space=pltpu.VMEM)
    hbm = pl.BlockSpec(memory_space=pl.ANY)
    return pl.pallas_call(
        gather_kernel,
        name="sketch_sums",
        out_shape=(pltpu.VMEM((RANK, OWN), F32), pltpu.VMEM((RANK, RANK), F32), pltpu.VMEM((256, 256), F32)),
        in_specs=[hbm, hbm, hbm],
        out_specs=(vmem, vmem, vmem),
        scratch_shapes=[
            bf(STEPS, RANK), bf(RANK, STEPS), bf(NY, STEPS, NZ * OWN), bf(NY, 256, NZ * OWN), fl(NZ, NY, RANK, OWN), fl(256, 256),
            bf(2, NZ, 2, A, HALF), bf(2, NZ, 2, A, HALF), bf(2, NZ, A, HALF), bf(2, NZ, A, HALF),
            bf(2, 4, 2, A, HALF), bf(2, 4, 2, A, HALF), bf(2, 4, 2, NY, B, HALF), bf(2, 4, 2, NY, B, HALF),
            bf(2, 2, B, HALF), bf(2, 2, B, HALF), bf(2, B, HALF), bf(2, B, HALF),
            fl(7, 32, 256), fl(256, 256),
            fl(RANK, RANK), fl(7, 16, RANK), fl(NY, 16, RANK), fl(NZ, 16, RANK), fl(RANK, RANK),
            dma((2, NY)), dma((2, 2, 5)), dma((2, 2, 5)), dma((2, 2, 4)), dma((2, 2, 4, 2)), dma((2, 2)), dma((2, 2)),
            dma((2, 7)), dma((2, NC)),
            dma((7,)), dma((7,)), dma((3,)), dma((NY,)), dma((7,)), dma((NZ,)), dma((7,)), dma((NC,)), dma((4,)),
        ],
        compiler_params=pltpu.CompilerParams(
            collective_id=1, has_side_effects=True, vmem_limit_bytes=60 << 20),
    )(state, range_test, corange_test)


def inverse_factor(w, scale):
    lane = lax.broadcasted_iota(jnp.int32, (8, RANK), 1)
    sub = lax.broadcasted_iota(jnp.int32, (8, RANK), 0)
    full = (8, RANK)
    out = []
    for b in range(RANK // 8):
        k = 8 * b
        inside = (lane >= k) & (lane < k + 8)
        cols = [jnp.broadcast_to(w[b][:, k + j:k + j + 1], full) for j in range(8)]
        p = [[jnp.broadcast_to(cols[j][i:i + 1], full) for j in range(i + 1)] for i in range(8)]
        l = [[None] * 8 for _ in range(8)]
        inv = []
        for j in range(8):
            inv.append(1.0 / p[j][j])
            for i in range(j + 1, 8):
                l[i][j] = p[i][j] * inv[j]
            for i in range(j + 1, 8):
                for m in range(j + 1, i + 1):
                    p[i][m] = p[i][m] - l[i][j] * p[m][j]
        own = jnp.where(inside, jnp.where(lane - k == sub, 1.0, 0.0), w[b])
        rows = []
        for i in range(8):
            r = jnp.broadcast_to(own[i:i + 1], full)
            for j in range(i):
                r = r - l[i][j] * rows[j]
            rows.append(r)
        done = jnp.zeros(full, F32)
        for i in range(8):
            done = jnp.where(sub == i, rows[i] * (scale * lax.rsqrt(p[i][i])), done)
        out.append(jnp.where(lane < k + 8, done, 0.0))
        for rb in range(b + 1, RANK // 8):
            q = []
            new = jnp.where(inside, 0.0, w[rb])
            for j in range(8):
                v = jnp.broadcast_to(w[rb][:, k + j:k + j + 1], full)
                for i in range(j):
                    v = v - q[i] * l[j][i]
                q.append(v)
            t = [(q[j] * inv[j]) * rows[j] for j in range(8)]
            w[rb] = new - (((t[0] + t[1]) + (t[2] + t[3])) + ((t[4] + t[5]) + (t[6] + t[7])))
    return jnp.concatenate(out, axis=0)


def factor_kernel(scale, gram, st, cor, out_hbm, cor_out, basis, w_ref, sem):
    store = pltpu.make_async_copy(cor, cor_out, sem.at[0])
    store.start()
    w = [gram[8 * b:8 * b + 8] for b in range(RANK // 8)]
    w_ref[...] = inverse_factor(w, scale)
    outs = []
    for h in (0, 1):
        basis[span(h)] = lax.dot_general(st[:, span(h)], w_ref[...], (((0,), (1,)), ((), ())),
                                         precision=lax.Precision.HIGHEST, preferred_element_type=F32)
        outs.append(pltpu.make_async_copy(basis.at[span(h)], out_hbm.at[span(h)], sem.at[1 + h]))
        outs[h].start()
    store.wait()
    for out in outs:
        out.wait()


def factor(gram, st, cor, scale):
    hbm = pl.BlockSpec(memory_space=pl.ANY)
    vmem = pl.BlockSpec(memory_space=pltpu.VMEM)
    return pl.pallas_call(
        functools.partial(factor_kernel, scale),
        name="factor",
        out_shape=(jax.ShapeDtypeStruct((OWN, RANK), F32), jax.ShapeDtypeStruct(cor.shape, F32)),
        in_specs=[vmem, vmem, vmem],
        out_specs=(hbm, hbm),
        scratch_shapes=[pltpu.VMEM((OWN, RANK), F32), pltpu.VMEM((RANK, RANK), F32), pltpu.SemaphoreType.DMA((3,))],
        compiler_params=pltpu.CompilerParams(vmem_limit_bytes=32 << 20),
    )(gram, st, cor)


def on_device(state, range_test, corange_test):
    total_cells = state.shape[1] * NC
    st, gram, corange = gather(state, range_test, corange_test)
    return factor(gram, st, corange, float(total_cells) ** 0.5)


def solution(mesh):
    return jax.shard_map(
        on_device,
        mesh=mesh,
        in_specs=(P("tm", "cell"), P("tm", None), P(None, "cell")),
        out_specs=(P(("cell", "tm"), None), P(None, "tm")),
        check_vma=False,
    )
```
